256 devices in a mesh: lat: 64 (over x_hi, y, z), lev: 4 (over x_lo, core).
Axes of the slice: x: 4 (x_hi: 2, x_lo: 2; x = x_hi * 2 + x_lo), y: 4, z: 8, core: 2. Of those that a mesh axis runs over, the one named last changes fastest.
Arguments:
- tracers: float32 [9, 16, 1474560], P(None, 'lev', 'lat'), may hold values from 0 to 1
- delp: float32 [16, 1474560], P('lev', 'lat'), may hold values from 0.8 to 1.2
- theta: float32 [16, 1474560], P('lev', 'lat'), may hold values from 0.8 to 1.2
- wind_x: float32 [16, 1474560], P('lev', 'lat'), may hold values from -0.04 to 0.04
- wind_y: float32 [16, 1474560], P('lev', 'lat'), may hold values from -0.04 to 0.04
- surface: float32 [1474560], P('lat'), may hold values from -6 to 6
- level_weight: float32 [16], replicated, may hold values from 0.5 to 2
Outputs:
- new_tracers: float32 [9, 16, 1474560], P(None, 'lev', 'lat')
- new_theta: float32 [16, 1474560], P('lev', 'lat')
- new_delp: float32 [16, 1474560], P('lev', 'lat')
- geopotential: float32 [16, 1474560], P('lev', 'lat')
The draws below stay inside these ranges and needn't reach their ends.
All inputs are finite; a program needn't handle non-finite values.
Results may differ from the reference program's by a relative error of at most 0.000023.
Values sent between devices are 32-bit elements; how exact they have to be, the bound alone decides.
No kernel may reach another device: no remote copies, remote signals or barrier semaphores. Data moves between devices by JAX's collectives and lax.ppermute only.
A program may use at most 256 MiB of HBM per device.

```python
import math
import jax
import jax.numpy as jnp
from jax import lax

NLON = 2880
NQ = 9
SUBSTEPS = 2
FPASS = 3
NLAT = 512
LEVELS = 16


def block_levels(stream_key, extent, shards, smallest, top_value):
    factor_of = 1.0
    for dim, parts in shards:
        heights = jax.random.uniform(jax.random.fold_in(jax.random.fold_in(stream_key, 6), dim), (parts,), jnp.float32, smallest / len(shards), top_value / len(shards))
        factor_of = factor_of * jnp.repeat(jnp.exp(heights), extent[dim] // parts).reshape((-1,) + (1,) * (len(extent) - 1 - dim))
    return factor_of


def centred(own_key, dims, scale, reach, cuts=(), kind=jnp.bfloat16):
    level = block_levels(own_key, dims, cuts, -0.22, 0.18) if cuts else 1.0
    values = jax.random.normal(own_key, dims, jnp.float32) * scale * level
    return jnp.minimum(jnp.maximum(values, -reach), reach).astype(kind)


def setup_inputs(seed: int = 0) -> dict:
    key_of = jax.random.split(jax.random.key(seed), 8)
    tracers = jnp.clip(1.0 * jax.random.uniform(key_of[0], (NQ, LEVELS, NLAT * NLON), jnp.float32) ** block_levels(key_of[0], (NQ, LEVELS, NLAT * NLON), ((1, 4), (2, 64)), -0.2, 0.2), 0.0, 1.0)
    delp = jnp.clip(0.8 + 0.40000004 * jax.random.uniform(key_of[1], (LEVELS, NLAT * NLON), jnp.float32) ** block_levels(key_of[1], (LEVELS, NLAT * NLON), ((0, 4), (1, 64)), -0.2, 0.2), 0.8, 1.2)
    theta = jnp.clip(0.8 + 0.40000004 * jax.random.uniform(key_of[2], (LEVELS, NLAT * NLON), jnp.float32) ** block_levels(key_of[2], (LEVELS, NLAT * NLON), ((0, 4), (1, 64)), -0.2, 0.2), 0.8, 1.2)
    wind_x = jnp.clip(jax.random.uniform(key_of[3], (LEVELS, NLAT * NLON), jnp.float32, -0.04, 0.04) * block_levels(key_of[3], (LEVELS, NLAT * NLON), ((0, 4), (1, 64)), -0.4, 0.0), -0.04, 0.04)
    wind_y = jnp.clip(jax.random.uniform(key_of[4], (LEVELS, NLAT * NLON), jnp.float32, -0.04, 0.04) * block_levels(key_of[4], (LEVELS, NLAT * NLON), ((0, 4), (1, 64)), -0.4, 0.0), -0.04, 0.04)
    surface = centred(key_of[5], (NLAT * NLON,), 1.0, 6.0, ((0, 64),), jnp.float32)
    level_weight = jnp.clip(jnp.exp(jax.random.uniform(key_of[6], (LEVELS,), jnp.float32, math.log(0.5), math.log(2.0))), 0.5, 2.0)
    return dict(tracers=tracers, delp=delp, theta=theta, wind_x=wind_x, wind_y=wind_y, surface=surface, level_weight=level_weight)


top_pressure = 1.0


def roll_lon(fields, shift_by):
    return jnp.roll(fields, shift_by, axis=-1)


def substep(fields, wind_east, wind_north, first_row, lat_total):
    count = fields.shape[2] - 4
    face_value = (7.0 * (fields[:, :, 1:count + 2] + fields[:, :, 2:count + 3])
                  - (fields[:, :, 0:count + 1] + fields[:, :, 3:count + 4])) / 12.0
    face_wind = 0.5 * (wind_north[:, :count + 1] + wind_north[:, 1:count + 2])
    row_index = first_row + jnp.arange(count + 1, dtype=jnp.int32)
    open_face = ((row_index > 0) & (row_index < lat_total)).astype(fields.dtype).reshape(1, 1, -1, 1)
    north_flux = open_face * face_wind[None] * face_value
    centre = fields[:, :, 2:count + 2]
    east_value = (7.0 * (roll_lon(centre, 1) + centre) - (roll_lon(centre, 2) + roll_lon(centre, -1))) / 12.0
    east_wind = 0.5 * (roll_lon(wind_east, 1) + wind_east)
    east_flux = east_wind[None] * east_value
    return centre - (north_flux[:, :, 1:] - north_flux[:, :, :-1]) - (roll_lon(east_flux, -1) - east_flux)


def strength(first_row, count, lat_total):
    row_index = (first_row + jnp.arange(count, dtype=jnp.int32)).astype(jnp.float32)
    latitude = jnp.pi * ((row_index + 0.5) / lat_total - 0.5)
    return jnp.maximum(0.0, 1.0 - 2.0 * jnp.cos(latitude))


def filter_rows(fields, damping):
    damping = damping.astype(fields.dtype).reshape(1, 1, -1, 1)
    for filter_pass in range(FPASS):
        fields = fields + 0.25 * damping * (roll_lon(fields, 1) + roll_lon(fields, -1) - 2.0 * fields)
    return fields


def remap(fields, level_weight, surface_part):
    thick = fields[0]
    density = fields[1:] / thick[None]
    source_edges = top_pressure + jnp.concatenate([jnp.zeros_like(thick[:1]), jnp.cumsum(thick, axis=0)], axis=0)
    weight_sum = jnp.concatenate([jnp.zeros((1,), level_weight.dtype), jnp.cumsum(level_weight)])
    fraction = (weight_sum / weight_sum[-1]).reshape((-1,) + (1,) * (thick.ndim - 1))
    surface_pressure = source_edges[-1]
    target_edges = top_pressure + fraction * (surface_pressure - top_pressure)
    target_thick = target_edges[1:] - target_edges[:-1]

    def remap_layer(accum, layer):
        layer_density, lower_edge, thickness = layer
        intersection = (jnp.minimum(jnp.maximum(target_edges[1:] - lower_edge, 0.0), thickness)
                   - jnp.minimum(jnp.maximum(target_edges[:-1] - lower_edge, 0.0), thickness))
        return accum + layer_density[:, None] * intersection[None], None

    start = jnp.zeros((density.shape[0],) + thick.shape, thick.dtype)
    accum, unused = lax.scan(remap_layer, start, (jnp.moveaxis(density, 1, 0), source_edges[:-1], thick))
    remapped = accum / target_thick[None]
    log_ratio = jnp.log(target_edges[1:] / target_edges[:-1])
    column_term = remapped[-1] * log_ratio
    geopotential = surface_part + jnp.cumsum(column_term[::-1], axis=0)[::-1]
    return jnp.concatenate([remapped, target_thick[None], geopotential[None]], axis=0)


def reference(tracers, delp, theta, wind_x, wind_y, surface, level_weight):
    tracers = tracers.reshape(NQ, LEVELS, NLAT, NLON)
    delp = delp.reshape(LEVELS, NLAT, NLON)
    theta = theta.reshape(LEVELS, NLAT, NLON)
    wind_x = wind_x.reshape(LEVELS, NLAT, NLON)
    wind_y = wind_y.reshape(LEVELS, NLAT, NLON)
    surface = surface.reshape(NLAT, NLON)
    fields = jnp.concatenate([delp[None], tracers * delp[None], (theta * delp)[None]], axis=0)
    wind_north = jnp.pad(wind_y, ((0, 0), (1, 1), (0, 0)))
    for substep_index in range(SUBSTEPS):
        padded = jnp.pad(fields, ((0, 0), (0, 0), (2, 2), (0, 0)))
        fields = substep(padded, wind_x, wind_north, 0, NLAT)
    fields = filter_rows(fields, strength(0, NLAT, NLAT))

    def one_row(layer):
        return remap(layer[0], level_weight, layer[1])

    columns_out = lax.map(one_row, (jnp.moveaxis(fields, 2, 0), surface))
    columns_out = jnp.moveaxis(columns_out, 0, 2)
    columns_out = columns_out.reshape(NQ + 3, LEVELS, NLAT * NLON)
    return columns_out[:NQ], columns_out[NQ], columns_out[NQ + 1], columns_out[NQ + 2]
```

```python
import functools

import jax
import jax.numpy as jnp
from jax import lax
from jax.experimental import pallas as pl
from jax.experimental.pallas import tpu as pltpu
from jax.sharding import PartitionSpec as P

NLON = 2880
WIDE = 2944
HALF = 4
ROWS = 8
LAYERS = 4
BLOCK = 2304
TOP = 1.0
VMEM_LIMIT = 40 * 1024 * 1024


def params(**extra):
    return pltpu.CompilerParams(vmem_limit_bytes=VMEM_LIMIT, **extra)


def cost(flops, nbytes):
    return pl.CostEstimate(flops=flops, bytes_accessed=nbytes, transcendentals=0)


def shift(x, by):
    return pltpu.roll(x, by % WIDE, 1)


def wrap(x, odd):
    if odd:
        x = shift(x, -64)
    lane = lax.broadcasted_iota(jnp.int32, (8, 128), 1)
    first, last = x[:, :128], x[:, WIDE - 128 :]
    ends = jnp.where(lane < 96, pltpu.roll(first, 64, 1), pltpu.roll(last, 64, 1))
    last = jnp.where(lane < 64, last, ends)
    return jnp.concatenate([x[:, : WIDE - 128], last], axis=1)


def piece(own, north, south, r):
    if r < HALF:
        source, j = north, r
    elif r < HALF + ROWS:
        source, j = own, r - HALF
    else:
        source, j = south, r - HALF - ROWS
    odd = j % 2
    return source(j * NLON - 64 * odd), odd


def advance(f_ref, a_ref, b_ref, g_ref, out_ref, count, offset):
    def face(i, carry):
        g_ref[i] = a_ref[i + offset] * (
            7.0 * (f_ref[i + 1] + f_ref[i + 2]) - (f_ref[i] + f_ref[i + 3])
        )
        return carry

    def row(i, carry):
        f = f_ref[i + 2]
        value = 7.0 * (shift(f, 1) + f) - (shift(f, 2) + shift(f, -1))
        east = b_ref[i + offset] * value
        out_ref[i] = f - (g_ref[i + 1] - g_ref[i]) - (shift(east, -1) - east)
        return carry

    lax.fori_loop(0, count + 1, face, 0)
    lax.fori_loop(0, count, row, 0)


def smooth(f_ref, k_ref):
    def row(i, carry):
        k = k_ref[i]

        @pl.when(k > 0.0)
        def _():
            f = f_ref[i]
            for _ in range(3):
                f = f + k * (shift(f, 1) + shift(f, -1) - 2.0 * f)
            f_ref[i] = f

        return carry

    lax.fori_loop(0, ROWS, row, 0)


def emit(f_ref, store):
    lane = lax.broadcasted_iota(jnp.int32, (8, 128), 1)
    for pair in range(ROWS // 2):
        even, odd = f_ref[2 * pair], shift(f_ref[2 * pair + 1], 64)
        base = pair * 2 * NLON
        store(base, even[:, : WIDE - 128])
        store(
            base + WIDE - 128,
            jnp.where(lane < 64, even[:, WIDE - 128 :], odd[:, :128]),
        )
        store(base + WIDE, odd[:, 128:])


def both(x):
    return jnp.concatenate([x, x], axis=0)


def prepare_kernel(
    lat_total, row_ref, k_ref, delp_ref, wx_ref, wy_ref, north_ref, south_ref,
    thick_ref, a_ref, b_ref, d_ref, r_ref, x_ref, g_ref, f1_ref, f2_ref,
):
    def load(ref, field, r):
        x, odd = piece(
            lambda s: ref[:, pl.ds(s, WIDE)],
            lambda s: north_ref[field, :, pl.ds(s, WIDE)],
            lambda s: south_ref[field, :, pl.ds(s, WIDE)],
            r,
        )
        return wrap(both(x), odd)

    first = row_ref[0]
    for r in range(1, 15):
        x_ref[r] = load(wy_ref, 2, r)
    for i in range(13):
        face = first + (i - 2)
        scale = jnp.where((face > 0) & (face < lat_total), 1.0 / 24.0, 0.0)
        a_ref[i] = scale * (x_ref[i + 1] + x_ref[i + 2])
    for r in range(2, 14):
        w = load(wx_ref, 1, r)
        b_ref[r - 2] = (1.0 / 24.0) * (shift(w, 1) + w)
    for r in range(16):
        d_ref[r] = load(delp_ref, 0, r)
    advance(d_ref, a_ref, b_ref, g_ref, f1_ref, 12, 0)
    advance(f1_ref, a_ref, b_ref, g_ref, f2_ref, 8, 2)
    smooth(f2_ref, k_ref)

    def store(base, x):
        thick_ref[:, pl.ds(base, x.shape[1])] = x[:LAYERS]

    emit(f2_ref, store)
    for i in range(ROWS):
        r_ref[i] = 1.0 / f2_ref[i]


def prepare(first_row, k, delp, wx, wy, north, south, lat_total):
    rows = lambda n: jax.ShapeDtypeStruct((n, 8, WIDE), jnp.float32)
    vmem = pl.BlockSpec(memory_space=pltpu.VMEM)
    smem = pl.BlockSpec(memory_space=pltpu.SMEM)
    return pl.pallas_call(
        functools.partial(prepare_kernel, lat_total),
        out_shape=[
            jax.ShapeDtypeStruct(delp.shape, jnp.float32),
            rows(13), rows(12), rows(16), rows(8),
        ],
        in_specs=[smem, smem] + [vmem] * 5,
        out_specs=[vmem] * 5,
        scratch_shapes=[
            pltpu.VMEM((n, 8, WIDE), jnp.float32) for n in (16, 13, 12, 8)
        ],
        compiler_params=params(),
        cost_estimate=cost(12_000_000, 8_000_000),
        name="prepare",
    )(first_row, k, delp, wx, wy, north, south)


def transport_kernel(
    start, k_ref, theta_ref, lower_ref, upper_ref, north_ref, south_ref,
    a_ref, b_ref, d_ref, r_ref, out_ref, f0_ref, g_ref, f1_ref, f2_ref,
):
    whole = pl.program_id(0) + start

    def lower(s):
        x = lower_ref[0, :, pl.ds(s, WIDE)]
        if start:
            return x
        return jnp.where(whole == 0, theta_ref[:, pl.ds(s, WIDE)], x)

    for r in range(16):
        x, odd = piece(
            lambda s: jnp.concatenate([lower(s), upper_ref[0, :, pl.ds(s, WIDE)]], axis=0),
            lambda s: jnp.concatenate(
                [north_ref[0, :, pl.ds(s, WIDE)], north_ref[1, :, pl.ds(s, WIDE)]], axis=0
            ),
            lambda s: jnp.concatenate(
                [south_ref[0, :, pl.ds(s, WIDE)], south_ref[1, :, pl.ds(s, WIDE)]], axis=0
            ),
            r,
        )
        f0_ref[r] = wrap(x, odd) * d_ref[r]
    advance(f0_ref, a_ref, b_ref, g_ref, f1_ref, 12, 0)
    advance(f1_ref, a_ref, b_ref, g_ref, f2_ref, 8, 2)
    smooth(f2_ref, k_ref)
    for i in range(ROWS):
        f2_ref[i] = f2_ref[i] * r_ref[i]

    def store(base, x):
        out_ref[0, :, pl.ds(base, x.shape[1])] = x[:LAYERS]
        out_ref[1, :, pl.ds(base, x.shape[1])] = x[LAYERS:]

    emit(f2_ref, store)


def transport(start, pairs, k, theta, tracers, north, south, a, b, d, r):
    cells = theta.shape[1]
    field = lambda index: pl.BlockSpec((1, LAYERS, cells), index)
    halo = pl.BlockSpec((2, LAYERS, HALF * NLON), lambda p: (p, 0, 0))
    vmem = pl.BlockSpec(memory_space=pltpu.VMEM)
    return pl.pallas_call(
        functools.partial(transport_kernel, start),
        grid=(pairs,),
        out_shape=jax.ShapeDtypeStruct((2 * pairs, LAYERS, cells), jnp.float32),
        in_specs=[
            pl.BlockSpec(memory_space=pltpu.SMEM),
            vmem,
            field(lambda p: (jnp.maximum(2 * (p + start) - 1, 0), 0, 0)),
            field(lambda p: (2 * (p + start), 0, 0)),
            halo, halo, vmem, vmem, vmem, vmem,
        ],
        out_specs=pl.BlockSpec((2, LAYERS, cells), lambda p: (p, 0, 0)),
        scratch_shapes=[
            pltpu.VMEM((n, 8, WIDE), jnp.float32) for n in (16, 13, 12, 8)
        ],
        compiler_params=params(),
        cost_estimate=cost(8_000_000 * pairs, 4_000_000 + 1_900_000 * pairs),
        name="transport",
    )(k, theta, tracers, tracers, north, south, a, b, d, r)


def edges_kernel(frac_ref, lev_ref, thick_ref, ov_ref, delp_ref, log_ref, flag_ref):
    width = thick_ref.shape[1]
    levels = thick_ref.shape[0]
    lev = lev_ref[0]
    edge = [jnp.full((1, width), TOP, jnp.float32)]
    for l in range(levels):
        edge.append(edge[-1] + thick_ref[l : l + 1])
    total = edge[levels] - TOP
    level = lax.broadcasted_iota(jnp.int32, (LAYERS, width), 0)
    low = jnp.zeros((LAYERS, width), jnp.float32)
    high = low
    for i in range(LAYERS):
        low = jnp.where(level == i, frac_ref[LAYERS * lev + i], low)
        high = jnp.where(level == i, frac_ref[LAYERS * lev + i + 1], high)
    low, high = TOP + low * total, TOP + high * total
    delp = high - low
    delp_ref[...] = delp
    log_ref[...] = jnp.log(high / low)
    inverse = 1.0 / delp
    none = jnp.zeros((LAYERS, width), jnp.float32)
    for l in range(LAYERS):
        ov_ref[l] = none
        ov_ref[l + LAYERS + levels] = none
    for l in range(levels):
        base = jnp.broadcast_to(edge[l], (LAYERS, width))
        limit = jnp.broadcast_to(thick_ref[l : l + 1], (LAYERS, width))
        part = jnp.minimum(jnp.maximum(high - base, 0.0), limit) - jnp.minimum(
            jnp.maximum(low - base, 0.0), limit
        )
        ov_ref[l + LAYERS] = part * inverse

    @pl.when(pl.program_id(0) == 0)
    def _():
        flag_ref[...] = jnp.full(flag_ref.shape, -1.0, jnp.float32)

    for reach in range(1, LAYERS + 1):
        worst = jnp.full((1, width), -1.0, jnp.float32)
        for m in range(LAYERS, levels, LAYERS):
            target = TOP + frac_ref[m] * total
            worst = jnp.maximum(worst, edge[m - reach] - target)
            worst = jnp.maximum(worst, target - edge[m + reach])
        best = worst[:, :128]
        for c in range(128, width, 128):
            best = jnp.maximum(best, worst[:, c : c + 128])
        flag_ref[reach - 1 : reach] = jnp.maximum(flag_ref[reach - 1 : reach], best)


def edges(frac, lev, thick):
    levels, cells = thick.shape
    smem = pl.BlockSpec(memory_space=pltpu.SMEM)
    own = pl.BlockSpec((LAYERS, BLOCK), lambda i: (0, i))
    return pl.pallas_call(
        edges_kernel,
        grid=(cells // BLOCK,),
        out_shape=[
            jax.ShapeDtypeStruct((levels + 2 * LAYERS, LAYERS, cells), jnp.float32),
            jax.ShapeDtypeStruct((LAYERS, cells), jnp.float32),
            jax.ShapeDtypeStruct((LAYERS, cells), jnp.float32),
            jax.ShapeDtypeStruct((8, 128), jnp.float32),
        ],
        in_specs=[smem, smem, pl.BlockSpec((levels, BLOCK), lambda i: (0, i))],
        out_specs=[
            pl.BlockSpec((levels + 2 * LAYERS, LAYERS, BLOCK), lambda i: (0, 0, i)),
            own, own, pl.BlockSpec((8, 128), lambda i: (0, 0)),
        ],
        compiler_params=params(),
        cost_estimate=cost(16_000_000, 11_000_000),
        name="edges",
    )(frac, lev, thick)


def mix(sources, field, width):
    total = None
    for density, overlap, first in sources:
        for l in range(density.shape[1]):
            x = jnp.broadcast_to(density[field, l : l + 1], (LAYERS, width))
            term = x * overlap[first + l]
            total = term if total is None else total + term
    return total


def remap_kernel(firsts, outer, groups_ref, *refs):
    n = len(firsts)
    densities, overlaps = refs[:n], refs[n : 2 * n]
    width = overlaps[0].shape[2]
    sources = list(zip(densities, overlaps, firsts))
    if outer:
        log_ref, surface_ref, theta_ref, tracer_ref, part_ref, sum_ref = refs[2 * n :]
        theta = mix(sources, 0, width)
        theta_ref[...] = theta
        column = theta * log_ref[...]
        partial = jnp.zeros((1, width), jnp.float32)
        surface = surface_ref[...]
        for k in range(LAYERS - 1, -1, -1):
            partial = partial + column[k : k + 1]
            part_ref[k : k + 1] = partial + surface
        sum_ref[...] = partial
        for q in range(1, densities[0].shape[0]):
            tracer_ref[q - 1] = mix(sources, q, width)
    else:
        tracer_ref = refs[-1]

        def field(q, carry):
            tracer_ref[q] = mix(sources, q, width)
            return carry

        lax.fori_loop(0, densities[0].shape[0], field, 0)


def remap(densities, groups, firsts, overlap, tracers, extra, shared=None):
    count, _, cells = densities[0].shape
    outer = shared is None
    step = count if outer else count // 2
    flat = lambda i, f, g: (0, i)
    density_spec = lambda d: pl.BlockSpec((step, d.shape[1], BLOCK), lambda i, f, g: (f, 0, i))
    overlap_spec = lambda c: pl.BlockSpec(
        (LAYERS, LAYERS, BLOCK), lambda i, f, g: (g[c], 0, i)
    )
    in_specs = [density_spec(d) for d in densities]
    in_specs += [overlap_spec(c) for c in range(len(densities))]
    args = list(densities) + [overlap] * len(densities)
    level = jax.ShapeDtypeStruct((LAYERS, cells), jnp.float32)
    whole = jax.ShapeDtypeStruct((tracers, LAYERS, cells), jnp.float32)
    aliases = {}
    if outer:
        args += list(extra)
        in_specs += [pl.BlockSpec((LAYERS, BLOCK), flat), pl.BlockSpec((1, BLOCK), flat)]
        out_shape = [level, whole, level, jax.ShapeDtypeStruct((1, cells), jnp.float32)]
        out_specs = [
            pl.BlockSpec((LAYERS, BLOCK), flat),
            pl.BlockSpec((count - 1, LAYERS, BLOCK), lambda i, f, g: (0, 0, i)),
            pl.BlockSpec((LAYERS, BLOCK), flat),
            pl.BlockSpec((1, BLOCK), flat),
        ]
    else:
        args += [shared]
        in_specs += [pl.BlockSpec(memory_space=pl.ANY)]
        aliases = {len(args): 0}
        out_shape = whole
        out_specs = pl.BlockSpec((step, LAYERS, BLOCK), lambda i, f, g: (f + 1, 0, i))
    kinds = sum(d.shape[1] for d in densities)
    return pl.pallas_call(
        functools.partial(remap_kernel, tuple(firsts), outer),
        grid_spec=pltpu.PrefetchScalarGridSpec(
            num_scalar_prefetch=1,
            grid=(cells // BLOCK, count // step),
            in_specs=in_specs,
            out_specs=out_specs,
        ),
        out_shape=out_shape,
        input_output_aliases=aliases,
        compiler_params=params(),
        cost_estimate=cost(
            count * kinds * LAYERS * cells * 2, cells * 4 * (count * (kinds + 4) + 48)
        ),
        name="remap",
    )(groups, *args)


def on_device(lat_total, tracers, delp, theta, wind_x, wind_y, surface, level_weight):
    count, layers, cells = tracers.shape
    bands, groups = lax.axis_size("lat"), lax.axis_size("lev")
    band, lev = lax.axis_index("lat"), lax.axis_index("lev")
    half = HALF * NLON
    to_south = [(i, i + 1) for i in range(bands - 1)]
    to_north = [(i + 1, i) for i in range(bands - 1)]

    def beside(parts):
        last = jnp.concatenate([p[:, :, half:] for p in parts], axis=0)
        leading = jnp.concatenate([p[:, :, :half] for p in parts], axis=0)
        return lax.ppermute(last, "lat", to_south), lax.ppermute(leading, "lat", to_north)

    first_row = (band * ROWS).astype(jnp.int32)
    row_index = (first_row + jnp.arange(ROWS, dtype=jnp.int32)).astype(jnp.float32)
    latitude = jnp.pi * ((row_index + 0.5) / lat_total - 0.5)
    k = 0.25 * jnp.maximum(0.0, 1.0 - 2.0 * jnp.cos(latitude))
    sums = jnp.concatenate([jnp.zeros((1,), level_weight.dtype), jnp.cumsum(level_weight)])
    frac = sums / sums[-1]

    north, south = beside([delp[None], wind_x[None], wind_y[None]])
    halos = [beside([theta[None], tracers[:3]]), beside([tracers[3:]])]
    thick, a, b, d, r = prepare(
        first_row[None], k, delp, wind_x, wind_y, north, south, lat_total
    )
    thick_all = lax.all_gather(thick, "lev", axis=0, tiled=True)
    overlap, new_delp, log_ratio, flags = edges(frac, lev[None], thick_all)
    density = [
        transport(start, pairs, k, theta, tracers, *halo, a, b, d, r)
        for start, pairs, halo in ((0, 2, halos[0]), (2, 3, halos[1]))
    ]
    fits = jnp.max(flags, axis=1) <= 0.0
    choice = jnp.where(fits[1], 0, jnp.where(fits[2], 1, jnp.where(fits[3], 2, 3)))

    down = lambda by: [(i + by, i) for i in range(groups - by)]
    up = lambda by: [(i, i + by) for i in range(groups - by)]

    def finish(gather, density, overlap, log_ratio, surface):
        sources = [gather(x) for x in density]
        new_theta, shared, partial, total = remap(
            *sources[0], overlap, count, (log_ratio, surface)
        )
        above = sum(lax.ppermute(total, "lev", down(by)) for by in range(1, groups))
        new_tracers = remap(*sources[1], overlap, count, None, shared)
        return new_tracers, new_theta, partial + above

    def near(reach):
        def gather(x):
            below = lax.ppermute(x[:, layers - reach :], "lev", up(1))
            above = lax.ppermute(x[:, :reach], "lev", down(1))
            return (x, below, above), lev + jnp.array([1, 0, 2]), (0, layers - reach, 0)

        return functools.partial(finish, gather)

    def far(density, overlap, log_ratio, surface):
        def gather(x):
            around = [x] + [
                lax.ppermute(x, "lev", [(i, (i + by) % groups) for i in range(groups)])
                for by in range(1, groups)
            ]
            owner = (lev - jnp.arange(groups)) % groups
            return tuple(around), owner + 1, (0,) * groups

        return finish(gather, density, overlap, log_ratio, surface)

    new_tracers, new_theta, geopotential = lax.switch(
        choice, [near(2), near(3), near(4), far], density, overlap, log_ratio, surface[None]
    )
    return new_tracers, new_theta, new_delp, geopotential


def solution(mesh):
    lat_total = ROWS * mesh.shape["lat"]
    return jax.shard_map(
        functools.partial(on_device, lat_total),
        mesh=mesh,
        in_specs=(
            P(None, "lev", "lat"),
            P("lev", "lat"),
            P("lev", "lat"),
            P("lev", "lat"),
            P("lev", "lat"),
            P("lat"),
            P(),
        ),
        out_specs=(P(None, "lev", "lat"), P("lev", "lat"), P("lev", "lat"), P("lev", "lat")),
        check_vma=False,
    )
```

```python
import functools

import jax
import jax.numpy as jnp
from jax import lax
from jax.experimental import pallas as pl
from jax.experimental.pallas import tpu as pltpu
from jax.sharding import PartitionSpec as P

NLON = 2880
WIDE = 2944
HALF = 4
ROWS = 8
LAYERS = 4
BLOCK = 3840
TOP = 1.0
SPLIT = 4
VMEM_LIMIT = 40 * 1024 * 1024


def params(**extra):
    return pltpu.CompilerParams(vmem_limit_bytes=VMEM_LIMIT, **extra)


SMALL = pl.CostEstimate(flops=1000, bytes_accessed=1000, transcendentals=0)


def shift(x, by):
    return pltpu.roll(x, by % WIDE, 1)


def wrap(x, odd):
    if odd:
        x = shift(x, -64)
    lane = lax.broadcasted_iota(jnp.int32, (8, 128), 1)
    first, last = x[:, :128], x[:, WIDE - 128 :]
    ends = jnp.where(lane < 96, pltpu.roll(first, 64, 1), pltpu.roll(last, 64, 1))
    last = jnp.where(lane < 64, last, ends)
    return jnp.concatenate([x[:, : WIDE - 128], last], axis=1)


def piece(own, north, south, r):
    if r < HALF:
        source, j = north, r
    elif r < HALF + ROWS:
        source, j = own, r - HALF
    else:
        source, j = south, r - HALF - ROWS
    odd = j % 2
    return source(j * NLON - 64 * odd), odd


def advance(f_ref, a_ref, b_ref, g_ref, out_ref, count, offset):
    def face(i, carry):
        g_ref[i] = a_ref[i + offset] * (
            7.0 * (f_ref[i + 1] + f_ref[i + 2]) - (f_ref[i] + f_ref[i + 3])
        )
        return carry

    def row(i, carry):
        f = f_ref[i + 2]
        value = 7.0 * (shift(f, 1) + f) - (shift(f, 2) + shift(f, -1))
        east = b_ref[i + offset] * value
        out_ref[i] = f - (g_ref[i + 1] - g_ref[i]) - (shift(east, -1) - east)
        return carry

    lax.fori_loop(0, count + 1, face, 0, unroll=True)
    lax.fori_loop(0, count, row, 0, unroll=True)


def smooth(f_ref, k_ref):
    def row(i, carry):
        k = k_ref[i]

        @pl.when(k > 0.0)
        def _():
            f = f_ref[i]
            for _ in range(3):
                f = f + k * (shift(f, 1) + shift(f, -1) - 2.0 * f)
            f_ref[i] = f

        return carry

    lax.fori_loop(0, ROWS, row, 0)


def emit(f_ref, store):
    lane = lax.broadcasted_iota(jnp.int32, (8, 128), 1)
    for pair in range(ROWS // 2):
        even, odd = f_ref[2 * pair], shift(f_ref[2 * pair + 1], 64)
        base = pair * 2 * NLON
        store(base, even[:, : WIDE - 128])
        store(
            base + WIDE - 128,
            jnp.where(lane < 64, even[:, WIDE - 128 :], odd[:, :128]),
        )
        store(base + WIDE, odd[:, 128:])


def both(x):
    return jnp.concatenate([x, x], axis=0)


def prepare_kernel(
    lat_total, row_ref, k_ref, delp_ref, wx_ref, wy_ref, north_ref, south_ref,
    thick_ref, a_ref, b_ref, d_ref, r_ref, x_ref, g_ref, f1_ref, f2_ref,
):
    def load(ref, field, r):
        x, odd = piece(
            lambda s: ref[:, pl.ds(s, WIDE)],
            lambda s: north_ref[field, :, pl.ds(s, WIDE)],
            lambda s: south_ref[field, :, pl.ds(s, WIDE)],
            r,
        )
        return wrap(both(x), odd)

    first = row_ref[0]
    for r in range(1, 15):
        x_ref[r] = load(wy_ref, 2, r)
    for i in range(13):
        face = first + (i - 2)
        scale = jnp.where((face > 0) & (face < lat_total), 1.0 / 24.0, 0.0)
        a_ref[i] = scale * (x_ref[i + 1] + x_ref[i + 2])
    for r in range(2, 14):
        w = load(wx_ref, 1, r)
        b_ref[r - 2] = (1.0 / 24.0) * (shift(w, 1) + w)
    for r in range(16):
        d_ref[r] = load(delp_ref, 0, r)
    advance(d_ref, a_ref, b_ref, g_ref, f1_ref, 12, 0)
    advance(f1_ref, a_ref, b_ref, g_ref, f2_ref, 8, 2)
    smooth(f2_ref, k_ref)

    def store(base, x):
        thick_ref[:, pl.ds(base, x.shape[1])] = x[:LAYERS]

    emit(f2_ref, store)
    for i in range(ROWS):
        r_ref[i] = 1.0 / f2_ref[i]


def whole(*shape):
    return pl.BlockSpec(shape, lambda *_: (0,) * len(shape))


def prepare(first_row, k, delp, wx, wy, north, south, lat_total):
    rows = (13, 12, 16, 8)
    flat = whole(*delp.shape)
    halo = whole(*north.shape)
    smem = pl.BlockSpec(memory_space=pltpu.SMEM)
    return pl.pallas_call(
        functools.partial(prepare_kernel, lat_total),
        grid=(1,),
        out_shape=[jax.ShapeDtypeStruct(delp.shape, jnp.float32)]
        + [jax.ShapeDtypeStruct((n, 8, WIDE), jnp.float32) for n in rows],
        in_specs=[smem, smem, flat, flat, flat, halo, halo],
        out_specs=[flat] + [whole(n, 8, WIDE) for n in rows],
        scratch_shapes=[
            pltpu.VMEM((n, 8, WIDE), jnp.float32) for n in (16, 13, 12, 8)
        ],
        compiler_params=params(),
        cost_estimate=SMALL,
        name="prepare",
    )(first_row, k, delp, wx, wy, north, south)


def transport_kernel(with_theta, *refs):
    if with_theta:
        theta_ref, *refs = refs
    (
        k_ref, lower_ref, upper_ref, north_ref, south_ref,
        a_ref, b_ref, d_ref, r_ref, out_ref, f0_ref, g_ref, f1_ref, f2_ref,
    ) = refs
    pair = pl.program_id(0)

    def lower(s):
        x = lower_ref[0, :, pl.ds(s, WIDE)]
        if not with_theta:
            return x
        return jnp.where(pair == 0, theta_ref[:, pl.ds(s, WIDE)], x)

    for r in range(16):
        x, odd = piece(
            lambda s: jnp.concatenate([lower(s), upper_ref[0, :, pl.ds(s, WIDE)]], axis=0),
            lambda s: jnp.concatenate(
                [north_ref[0, :, pl.ds(s, WIDE)], north_ref[1, :, pl.ds(s, WIDE)]], axis=0
            ),
            lambda s: jnp.concatenate(
                [south_ref[0, :, pl.ds(s, WIDE)], south_ref[1, :, pl.ds(s, WIDE)]], axis=0
            ),
            r,
        )
        f0_ref[r] = wrap(x, odd) * d_ref[r]
    advance(f0_ref, a_ref, b_ref, g_ref, f1_ref, 12, 0)
    advance(f1_ref, a_ref, b_ref, g_ref, f2_ref, 8, 2)
    smooth(f2_ref, k_ref)
    for i in range(ROWS):
        f2_ref[i] = f2_ref[i] * r_ref[i]

    def store(base, x):
        out_ref[0, :, pl.ds(base, x.shape[1])] = x[:LAYERS]
        out_ref[1, :, pl.ds(base, x.shape[1])] = x[LAYERS:]

    emit(f2_ref, store)


def transport(pairs, first, theta, k, tracers, north, south, a, b, d, r):
    cells = tracers.shape[2]
    lead = 0 if theta is None else 1
    field = lambda index: pl.BlockSpec((1, LAYERS, cells), index)
    halo = pl.BlockSpec((2, LAYERS, HALF * NLON), lambda p: (p, 0, 0))
    rows = [whole(n, 8, WIDE) for n in (13, 12, 16, 8)]
    in_specs = [
        pl.BlockSpec(memory_space=pltpu.SMEM),
        field(lambda p: (jnp.maximum(first + 2 * p - lead, first), 0, 0)),
        field(lambda p: (first + 2 * p + 1 - lead, 0, 0)),
        halo, halo, *rows,
    ]
    args = [k, tracers, tracers, north, south, a, b, d, r]
    if lead:
        in_specs = [whole(*theta.shape)] + in_specs
        args = [theta] + args
    return pl.pallas_call(
        functools.partial(transport_kernel, bool(lead)),
        grid=(pairs,),
        out_shape=jax.ShapeDtypeStruct((2 * pairs, LAYERS, cells), jnp.float32),
        in_specs=in_specs,
        out_specs=pl.BlockSpec((2, LAYERS, cells), lambda p: (p, 0, 0)),
        scratch_shapes=[
            pltpu.VMEM((n, 8, WIDE), jnp.float32) for n in (16, 13, 12, 8)
        ],
        compiler_params=params(),
        cost_estimate=SMALL,
        name="transport",
    )(*args)


def edges_kernel(frac_ref, lev_ref, thick_ref, ov_ref, delp_ref, log_ref, flag_ref):
    width = thick_ref.shape[1]
    levels = thick_ref.shape[0]
    lev = lev_ref[0]
    edge = [jnp.full((1, width), TOP, jnp.float32)]
    for l in range(levels):
        edge.append(edge[-1] + thick_ref[l : l + 1])
    total = edge[levels] - TOP
    level = lax.broadcasted_iota(jnp.int32, (LAYERS, width), 0)
    low = jnp.zeros((LAYERS, width), jnp.float32)
    high = low
    for i in range(LAYERS):
        low = jnp.where(level == i, frac_ref[LAYERS * lev + i], low)
        high = jnp.where(level == i, frac_ref[LAYERS * lev + i + 1], high)
    low, high = TOP + low * total, TOP + high * total
    delp = high - low
    delp_ref[...] = delp
    log_ref[...] = jnp.log(high / low)
    inverse = 1.0 / delp
    none = jnp.zeros((LAYERS, width), jnp.float32)
    for l in range(LAYERS):
        ov_ref[l] = none
        ov_ref[l + LAYERS + levels] = none
    for l in range(levels):
        base = jnp.broadcast_to(edge[l], (LAYERS, width))
        limit = jnp.broadcast_to(thick_ref[l : l + 1], (LAYERS, width))
        part = jnp.minimum(jnp.maximum(high - base, 0.0), limit) - jnp.minimum(
            jnp.maximum(low - base, 0.0), limit
        )
        ov_ref[l + LAYERS] = part * inverse

    @pl.when(pl.program_id(0) == 0)
    def _():
        flag_ref[...] = jnp.full(flag_ref.shape, -1.0, jnp.float32)

    for reach in range(1, LAYERS + 1):
        worst = jnp.full((1, width), -1.0, jnp.float32)
        for m in range(LAYERS, levels, LAYERS):
            target = TOP + frac_ref[m] * total
            worst = jnp.maximum(worst, edge[m - reach] - target)
            worst = jnp.maximum(worst, target - edge[m + reach])
        best = worst[:, :128]
        for c in range(128, width, 128):
            best = jnp.maximum(best, worst[:, c : c + 128])
        flag_ref[reach - 1 : reach] = jnp.maximum(flag_ref[reach - 1 : reach], best)


def edges(frac, lev, thick):
    levels, cells = thick.shape
    smem = pl.BlockSpec(memory_space=pltpu.SMEM)
    own = pl.BlockSpec((LAYERS, BLOCK), lambda i: (0, i))
    return pl.pallas_call(
        edges_kernel,
        grid=(cells // BLOCK,),
        out_shape=[
            jax.ShapeDtypeStruct((levels + 2 * LAYERS, LAYERS, cells), jnp.float32),
            jax.ShapeDtypeStruct((LAYERS, cells), jnp.float32),
            jax.ShapeDtypeStruct((LAYERS, cells), jnp.float32),
            jax.ShapeDtypeStruct((8, 128), jnp.float32),
        ],
        in_specs=[smem, smem, pl.BlockSpec((levels, BLOCK), lambda i: (0, i))],
        out_specs=[
            pl.BlockSpec((levels + 2 * LAYERS, LAYERS, BLOCK), lambda i: (0, 0, i)),
            own, own, pl.BlockSpec((8, 128), lambda i: (0, 0)),
        ],
        compiler_params=params(),
        cost_estimate=SMALL,
        name="edges",
    )(frac, lev, thick)


def mix(sources, field, width):
    total = None
    for density, overlap, first in sources:
        for l in range(density.shape[1]):
            x = jnp.broadcast_to(density[field, l : l + 1], (LAYERS, width))
            term = x * overlap[first + l]
            total = term if total is None else total + term
    return total


def remap_kernel(firsts, outer, groups_ref, *refs):
    n = len(firsts)
    densities, overlaps = refs[:n], refs[n : 2 * n]
    width = overlaps[0].shape[2]
    sources = list(zip(densities, overlaps, firsts))
    if outer:
        log_ref, surface_ref, theta_ref, tracer_ref, part_ref, sum_ref = refs[2 * n :]
        theta = mix(sources, 0, width)
        theta_ref[...] = theta
        column = theta * log_ref[...]
        partial = jnp.zeros((1, width), jnp.float32)
        surface = surface_ref[...]
        for k in range(LAYERS - 1, -1, -1):
            partial = partial + column[k : k + 1]
            part_ref[k : k + 1] = partial + surface
        sum_ref[...] = partial
        skip = tracer_ref.shape[0] - densities[0].shape[0]
        for q in range(1, densities[0].shape[0]):
            tracer_ref[q + skip] = mix(sources, q, width)
    else:
        tracer_ref = refs[-1]
        for q in range(densities[0].shape[0]):
            tracer_ref[q] = mix(sources, q, width)


def remap(densities, groups, firsts, overlap, tracers, extra, shared=None):
    count, _, cells = densities[0].shape
    flat = lambda i, g: (0, i)
    deep = lambda i, g: (0, 0, i)
    density_spec = lambda d: pl.BlockSpec((count, d.shape[1], BLOCK), deep)
    overlap_spec = lambda c: pl.BlockSpec((LAYERS, LAYERS, BLOCK), lambda i, g: (g[c], 0, i))
    in_specs = [density_spec(d) for d in densities]
    in_specs += [overlap_spec(c) for c in range(len(densities))]
    args = list(densities) + [overlap] * len(densities)
    level = jax.ShapeDtypeStruct((LAYERS, cells), jnp.float32)
    result = jax.ShapeDtypeStruct((tracers, LAYERS, cells), jnp.float32)
    aliases = {}
    if extra:
        args += list(extra)
        in_specs += [pl.BlockSpec((LAYERS, BLOCK), flat), pl.BlockSpec((1, BLOCK), flat)]
        out_shape = [level, result, level, jax.ShapeDtypeStruct((1, cells), jnp.float32)]
        out_specs = [
            pl.BlockSpec((LAYERS, BLOCK), flat),
            pl.BlockSpec((tracers, LAYERS, BLOCK), deep),
            pl.BlockSpec((LAYERS, BLOCK), flat),
            pl.BlockSpec((1, BLOCK), flat),
        ]
    else:
        args += [shared]
        in_specs += [pl.BlockSpec(memory_space=pl.ANY)]
        aliases = {len(args): 0}
        out_shape = result
        out_specs = pl.BlockSpec((count, LAYERS, BLOCK), deep)
    return pl.pallas_call(
        functools.partial(remap_kernel, tuple(firsts), bool(extra)),
        grid_spec=pltpu.PrefetchScalarGridSpec(
            num_scalar_prefetch=1,
            grid=(cells // BLOCK,),
            in_specs=in_specs,
            out_specs=out_specs,
        ),
        out_shape=out_shape,
        input_output_aliases=aliases,
        compiler_params=params(),
        cost_estimate=SMALL,
        name="remap",
    )(groups, *args)


def on_device(lat_total, tracers, delp, theta, wind_x, wind_y, surface, level_weight):
    count, layers, cells = tracers.shape
    bands, groups = lax.axis_size("lat"), lax.axis_size("lev")
    band, lev = lax.axis_index("lat"), lax.axis_index("lev")
    half = HALF * NLON
    to_south = [(i, i + 1) for i in range(bands - 1)]
    to_north = [(i + 1, i) for i in range(bands - 1)]

    def beside(parts):
        last = jnp.concatenate([p[:, :, half:] for p in parts], axis=0)
        leading = jnp.concatenate([p[:, :, :half] for p in parts], axis=0)
        return lax.ppermute(last, "lat", to_south), lax.ppermute(leading, "lat", to_north)

    first_row = (band * ROWS).astype(jnp.int32)
    row_index = (first_row + jnp.arange(ROWS, dtype=jnp.int32)).astype(jnp.float32)
    latitude = jnp.pi * ((row_index + 0.5) / lat_total - 0.5)
    k = 0.25 * jnp.maximum(0.0, 1.0 - 2.0 * jnp.cos(latitude))
    sums = jnp.concatenate([jnp.zeros((1,), level_weight.dtype), jnp.cumsum(level_weight)])
    frac = sums / sums[-1]

    north, south = beside([delp[None], wind_x[None], wind_y[None]])
    halo_one = beside([theta[None], tracers[SPLIT:]])
    halo_two = beside([tracers[:SPLIT]])
    thick, *rows = prepare(
        first_row[None], k, delp, wind_x, wind_y, north, south, lat_total
    )
    thick_all = lax.all_gather(thick, "lev", axis=0, tiled=True)
    one = transport((count - SPLIT + 1) // 2, SPLIT, theta, k, tracers, *halo_one, *rows)
    overlap, new_delp, log_ratio, flags = edges(frac, lev[None], thick_all)
    fits = jnp.max(flags, axis=1) <= 0.0
    choice = jnp.where(fits[1], 2, jnp.where(fits[2], 1, 0))

    down = lambda by: [(i + by, i) for i in range(groups - by)]
    up = lambda by: [(i, i + by) for i in range(groups - by)]

    def finish(gather, one, overlap, log_ratio, surface, k, tracers, halo_two, rows):
        source_one = gather(one)
        two = transport(SPLIT // 2, 0, None, k, tracers, *halo_two, *rows)
        source_two = gather(two)
        new_theta, shared, partial, total = remap(
            *source_one, overlap, count, (log_ratio, surface)
        )
        above = sum(lax.ppermute(total, "lev", down(by)) for by in range(1, groups))
        new_tracers = remap(*source_two, overlap, count, None, shared)
        return new_tracers, new_theta, partial + above

    def near(reach):
        def gather(x):
            below = lax.ppermute(x[:, layers - reach :], "lev", up(1))
            above = lax.ppermute(x[:, :reach], "lev", down(1))
            return (x, below, above), lev + jnp.array([1, 0, 2]), (0, layers - reach, 0)

        return functools.partial(finish, gather)

    def far(*operands):
        def gather(x):
            around = [x] + [
                lax.ppermute(x, "lev", [(i, (i + by) % groups) for i in range(groups)])
                for by in range(1, groups)
            ]
            owner = (lev - jnp.arange(groups)) % groups
            return tuple(around), owner + 1, (0,) * groups

        return finish(gather, *operands)

    new_tracers, new_theta, geopotential = lax.switch(
        choice,
        [far, near(3), near(2)],
        one, overlap, log_ratio, surface[None], k, tracers, halo_two, rows,
    )
    return new_tracers, new_theta, new_delp, geopotential


def solution(mesh):
    lat_total = ROWS * mesh.shape["lat"]
    return jax.shard_map(
        functools.partial(on_device, lat_total),
        mesh=mesh,
        in_specs=(
            P(None, "lev", "lat"),
            P("lev", "lat"),
            P("lev", "lat"),
            P("lev", "lat"),
            P("lev", "lat"),
            P("lat"),
            P(),
        ),
        out_specs=(P(None, "lev", "lat"), P("lev", "lat"), P("lev", "lat"), P("lev", "lat")),
        check_vma=False,
    )
```

```python
import functools

import jax
import jax.numpy as jnp
from jax import lax
from jax.experimental import pallas as pl
from jax.experimental.pallas import tpu as pltpu
from jax.sharding import PartitionSpec as P

NLON = 2880
WIDE = 2944
HALF = 4
ROWS = 8
LAYERS = 4
BLOCK = 3840
TOP = 1.0
ROW_UNROLL = 4
SMOOTH_UNROLL = 4
PAIR_UNROLL = 2
SPLIT = 4
VMEM_LIMIT = 60 * 1024 * 1024


def params(**extra):
    return pltpu.CompilerParams(vmem_limit_bytes=VMEM_LIMIT, **extra)


SMALL = pl.CostEstimate(flops=1000, bytes_accessed=1000, transcendentals=0)


def shift(x, by):
    return pltpu.roll(x, by % WIDE, 1)


def wrap(x, odd):
    if odd:
        x = shift(x, -64)
    lane = lax.broadcasted_iota(jnp.int32, (8, 128), 1)
    first, last = x[:, :128], x[:, WIDE - 128 :]
    ends = jnp.where(lane < 96, pltpu.roll(first, 64, 1), pltpu.roll(last, 64, 1))
    last = jnp.where(lane < 64, last, ends)
    return jnp.concatenate([x[:, : WIDE - 128], last], axis=1)


def widen(own, north, south, put):
    def pairs(source, count, first):
        def pair(i, carry):
            base = pl.multiple_of(i * (2 * NLON), 128)
            put(first + 2 * i, wrap(source(base), False))
            put(first + 2 * i + 1, wrap(source(base + NLON - 64), True))
            return carry

        lax.fori_loop(0, count, pair, 0, unroll=PAIR_UNROLL)

    pairs(north, HALF // 2, 0)
    pairs(own, ROWS // 2, HALF)
    pairs(south, HALF // 2, HALF + ROWS)


def advance(f_ref, a_ref, b_ref, c_ref, out_ref, count, offset):
    def face(i):
        return a_ref[i + offset] * (
            7.0 * (f_ref[i + 1] + f_ref[i + 2]) - (f_ref[i] + f_ref[i + 3])
        )

    def row(i, carry):
        f = f_ref[i + 2]
        west, east = shift(f, 1), shift(f, -1)
        west_flux = b_ref[i + offset] * (7.0 * (west + f) - (shift(f, 2) + east))
        east_flux = c_ref[i + offset] * (7.0 * (f + east) - (west + shift(f, -2)))
        out_ref[i] = f - (face(i + 1) - face(i)) - (east_flux - west_flux)
        return carry

    lax.fori_loop(0, count, row, 0, unroll=ROW_UNROLL)


def smooth(f_ref, k_ref):
    def row(i, carry):
        k = k_ref[i]
        keep = 1.0 - 2.0 * k
        f = f_ref[i]
        near = shift(f, 1) + shift(f, -1)
        middle = shift(f, 2) + shift(f, -2)
        outer = shift(f, 3) + shift(f, -3)
        f_ref[i] = (
            (keep * keep * keep + 6.0 * keep * k * k) * f
            + (3.0 * keep * keep * k + 3.0 * k * k * k) * near
            + (3.0 * keep * k * k) * middle
            + (k * k * k) * outer
        )
        return carry

    largest = k_ref[0]
    for i in range(1, ROWS):
        largest = jnp.maximum(largest, k_ref[i])

    @pl.when(largest > 0.0)
    def _():
        lax.fori_loop(0, ROWS, row, 0, unroll=SMOOTH_UNROLL)


def emit(f_ref, store, scale_ref=None):
    lane = lax.broadcasted_iota(jnp.int32, (8, 128), 1)

    def pair(i, carry):
        even, odd = f_ref[2 * i], f_ref[2 * i + 1]
        if scale_ref is not None:
            even, odd = even * scale_ref[2 * i], odd * scale_ref[2 * i + 1]
        odd = shift(odd, 64)
        middle = jnp.where(lane < 64, even[:, WIDE - 128 :], odd[:, :128])
        base = pl.multiple_of(i * (2 * NLON), 128)
        store(base, jnp.concatenate([even[:, : WIDE - 128], middle, odd[:, 128:]], axis=1))
        return carry

    lax.fori_loop(0, ROWS // 2, pair, 0, unroll=PAIR_UNROLL)


def both(x):
    return jnp.concatenate([x, x], axis=0)


def prepare_kernel(
    lat_total, row_ref, k_ref, delp_ref, wx_ref, wy_ref, north_ref, south_ref,
    thick_ref, a_ref, b_ref, c_ref, d_ref, r_ref, x_ref, f1_ref, f2_ref,
):
    def load(ref, field, put):
        widen(
            lambda at: both(ref[:, pl.ds(at, WIDE)]),
            lambda at: both(north_ref[field, :, pl.ds(at, WIDE)]),
            lambda at: both(south_ref[field, :, pl.ds(at, WIDE)]),
            put,
        )

    first = row_ref[0]

    def put_x(r, x):
        x_ref[r] = x

    def put_d(r, x):
        d_ref[r] = x

    load(wy_ref, 2, put_x)

    def face(i, carry):
        at = first + (i - 2)
        scale = jnp.where((at > 0) & (at < lat_total), 1.0 / 24.0, 0.0)
        a_ref[i] = scale * (x_ref[i + 1] + x_ref[i + 2])
        return carry

    lax.fori_loop(0, 13, face, 0)
    load(wx_ref, 1, put_x)

    def east(i, carry):
        w = x_ref[i + 2]
        b_ref[i] = (1.0 / 24.0) * (shift(w, 1) + w)
        c_ref[i] = (1.0 / 24.0) * (w + shift(w, -1))
        return carry

    lax.fori_loop(0, 12, east, 0, unroll=2)
    load(delp_ref, 0, put_d)
    advance(d_ref, a_ref, b_ref, c_ref, f1_ref, 12, 0)
    advance(f1_ref, a_ref, b_ref, c_ref, f2_ref, 8, 2)
    smooth(f2_ref, k_ref)

    def store(base, x):
        thick_ref[:, pl.ds(base, x.shape[1])] = x[:LAYERS]

    emit(f2_ref, store)

    def invert(i, carry):
        r_ref[i] = 1.0 / f2_ref[i]
        return carry

    lax.fori_loop(0, ROWS, invert, 0)


def whole(*shape):
    return pl.BlockSpec(shape, lambda *_: (0,) * len(shape))


def prepare(first_row, k, delp, wx, wy, north, south, lat_total):
    rows = (13, 12, 12, 16, 8)
    flat = whole(*delp.shape)
    halo = whole(*north.shape)
    smem = pl.BlockSpec(memory_space=pltpu.SMEM)
    return pl.pallas_call(
        functools.partial(prepare_kernel, lat_total),
        grid=(1,),
        out_shape=[jax.ShapeDtypeStruct(delp.shape, jnp.float32)]
        + [jax.ShapeDtypeStruct((n, 8, WIDE), jnp.float32) for n in rows],
        in_specs=[smem, smem, flat, flat, flat, halo, halo],
        out_specs=[flat] + [whole(n, 8, WIDE) for n in rows],
        scratch_shapes=[
            pltpu.VMEM((n, 8, WIDE), jnp.float32) for n in (16, 12, 8)
        ],
        compiler_params=params(),
        cost_estimate=SMALL,
        name="prepare",
    )(first_row, k, delp, wx, wy, north, south)


def transport_kernel(with_theta, *refs):
    if with_theta:
        theta_ref, *refs = refs
    (
        k_ref, lower_ref, upper_ref, north_ref, south_ref,
        a_ref, b_ref, c_ref, d_ref, r_ref, first_ref, last_ref, f0_ref, f1_ref, f2_ref,
    ) = refs
    pair = pl.program_id(0)

    def lower(s):
        x = lower_ref[0, :, pl.ds(s, WIDE)]
        if not with_theta:
            return x
        return jnp.where(pair == 0, theta_ref[:, pl.ds(s, WIDE)], x)

    def put(r, x):
        f0_ref[r] = x * d_ref[r]

    widen(
        lambda at: jnp.concatenate([lower(at), upper_ref[0, :, pl.ds(at, WIDE)]], axis=0),
        lambda at: jnp.concatenate(
            [north_ref[0, :, pl.ds(at, WIDE)], north_ref[1, :, pl.ds(at, WIDE)]], axis=0
        ),
        lambda at: jnp.concatenate(
            [south_ref[0, :, pl.ds(at, WIDE)], south_ref[1, :, pl.ds(at, WIDE)]], axis=0
        ),
        put,
    )
    advance(f0_ref, a_ref, b_ref, c_ref, f1_ref, 12, 0)
    advance(f1_ref, a_ref, b_ref, c_ref, f2_ref, 8, 2)
    smooth(f2_ref, k_ref)

    def store(base, x):
        at = pl.ds(base, x.shape[1])
        for field in range(2):
            first_ref[field, :, at] = x[LAYERS * field : LAYERS * field + 2]
            last_ref[field, :, at] = x[LAYERS * field + 2 : LAYERS * field + 4]

    emit(f2_ref, store, r_ref)


def transport(pairs, first, theta, k, tracers, north, south, *rows):
    cells = tracers.shape[2]
    lead = 0 if theta is None else 1
    field = lambda index: pl.BlockSpec((1, LAYERS, cells), index)
    halo = pl.BlockSpec((2, LAYERS, HALF * NLON), lambda p: (p, 0, 0))
    in_specs = [
        pl.BlockSpec(memory_space=pltpu.SMEM),
        field(lambda p: (jnp.maximum(first + 2 * p - lead, first), 0, 0)),
        field(lambda p: (first + 2 * p + 1 - lead, 0, 0)),
        halo, halo, *[whole(*x.shape) for x in rows],
    ]
    args = [k, tracers, tracers, north, south, *rows]
    half = pl.BlockSpec((2, 2, cells), lambda p: (p, 0, 0))
    if lead:
        in_specs = [whole(*theta.shape)] + in_specs
        args = [theta] + args
    return pl.pallas_call(
        functools.partial(transport_kernel, bool(lead)),
        grid=(pairs,),
        out_shape=[jax.ShapeDtypeStruct((2 * pairs, 2, cells), jnp.float32)] * 2,
        in_specs=in_specs,
        out_specs=[half, half],
        scratch_shapes=[
            pltpu.VMEM((n, 8, WIDE), jnp.float32) for n in (16, 12, 8)
        ],
        compiler_params=params(),
        cost_estimate=SMALL,
        name="transport",
    )(*args)


def edges_kernel(
    rows, weight_ref, lev_ref, thick_ref,
    ov_ref, delp_ref, log_ref, choice_ref, edge_ref, flag_ref,
):
    wrapped, places = rows
    groups, _, width = thick_ref.shape
    levels = groups * LAYERS
    lev = lev_ref[0]
    sums = [jnp.float32(0.0)]
    for l in range(levels):
        sums.append(sums[-1] + weight_ref[l])
    edge = jnp.full((1, width), TOP, jnp.float32)
    marks = []
    for l in range(levels):
        edge_ref[l // LAYERS, l % LAYERS : l % LAYERS + 1] = edge
        marks.append(edge)
        edge = edge + thick_ref[l // LAYERS, l % LAYERS : l % LAYERS + 1]
    scale = (edge - TOP) / jnp.full((1, width), sums[levels], jnp.float32)
    level = lax.broadcasted_iota(jnp.int32, (LAYERS, width), 0)
    low = jnp.zeros((LAYERS, width), jnp.float32)
    high = low
    own = [sums[i] for i in range(LAYERS + 1)]
    for g in range(1, groups):
        own = [jnp.where(lev == g, sums[g * LAYERS + i], own[i]) for i in range(LAYERS + 1)]
    for i in range(LAYERS):
        low = jnp.where(level == i, own[i], low)
        high = jnp.where(level == i, own[i + 1], high)
    low, high = TOP + low * scale, TOP + high * scale
    delp = high - low
    delp_ref[...] = delp
    log_ref[...] = jnp.log(high / low)
    inverse = 1.0 / delp
    for i, (away, l) in enumerate(places):
        if wrapped:
            group = lax.rem(lev + away + groups, groups)
        else:
            group = jnp.clip(lev + away, 0, groups - 1)
        base = jnp.broadcast_to(edge_ref[group, l : l + 1], (LAYERS, width))
        limit = jnp.broadcast_to(thick_ref[group, l : l + 1], (LAYERS, width))
        part = jnp.minimum(jnp.maximum(high - base, 0.0), limit) - jnp.minimum(
            jnp.maximum(low - base, 0.0), limit
        )
        ov_ref[i] = part * inverse

    step = pl.program_id(0)

    @pl.when(step == 0)
    def _():
        flag_ref[...] = jnp.full(flag_ref.shape, -1.0, jnp.float32)

    worst = [None, None]
    for m in range(LAYERS, levels, LAYERS):
        target = TOP + sums[m] * scale
        for i in range(2):
            over = jnp.maximum(marks[m - 2 - i] - target, target - marks[m + 2 + i])
            worst[i] = over if worst[i] is None else jnp.maximum(worst[i], over)
    for i in range(2):
        best = worst[i][:, :128]
        for c in range(128, width, 128):
            best = jnp.maximum(best, worst[i][:, c : c + 128])
        flag_ref[i : i + 1] = jnp.maximum(flag_ref[i : i + 1], best)

    @pl.when(step == pl.num_programs(0) - 1)
    def _():
        two, three = jnp.max(flag_ref[0:1]), jnp.max(flag_ref[1:2])
        choice_ref[0] = jnp.where(two <= 0.0, 0, jnp.where(three <= 0.0, 1, 2))


def edges(weight, lev, thick, rows):
    groups, _, cells = thick.shape
    count = len(rows[1])
    smem = pl.BlockSpec(memory_space=pltpu.SMEM)
    own = pl.BlockSpec((LAYERS, BLOCK), lambda i: (0, i))
    level = jax.ShapeDtypeStruct((LAYERS, cells), jnp.float32)
    return pl.pallas_call(
        functools.partial(edges_kernel, rows),
        grid=(cells // BLOCK,),
        out_shape=[
            jax.ShapeDtypeStruct((count, LAYERS, cells), jnp.float32),
            level, level, jax.ShapeDtypeStruct((1,), jnp.int32),
        ],
        in_specs=[smem, smem, pl.BlockSpec((groups, LAYERS, BLOCK), lambda i: (0, 0, i))],
        out_specs=[
            pl.BlockSpec((count, LAYERS, BLOCK), lambda i: (0, 0, i)),
            own, own, smem,
        ],
        scratch_shapes=[
            pltpu.VMEM((groups, LAYERS, BLOCK), jnp.float32),
            pltpu.VMEM((8, 128), jnp.float32),
        ],
        compiler_params=params(),
        cost_estimate=SMALL,
        name="edges",
    )(weight, lev, thick)


def mix(sources, firsts, ov_ref, field):
    width = ov_ref.shape[2]
    total = None
    for density, first in zip(sources, firsts):
        for l in range(density.shape[1]):
            x = jnp.broadcast_to(density[field, l : l + 1], (LAYERS, width))
            term = x * ov_ref[first + l]
            total = term if total is None else total + term
    return total


def theta_kernel(firsts, *refs):
    n = len(firsts)
    ov_ref, log_ref, surface_ref, theta_ref, part_ref, sum_ref = refs[n:]
    theta = mix(refs[:n], firsts, ov_ref, 0)
    theta_ref[...] = theta
    column = theta * log_ref[...]
    partial = jnp.zeros((1, column.shape[1]), jnp.float32)
    for k in range(LAYERS - 1, -1, -1):
        partial = partial + column[k : k + 1]
        part_ref[k : k + 1] = partial + surface_ref[...]
    sum_ref[...] = partial


def tracer_kernel(firsts, *refs):
    n = len(firsts)
    one, two, ov_ref, out_ref = refs[:n], refs[n : 2 * n], refs[-2], refs[-1]
    for q in range(SPLIT):
        out_ref[q] = mix(two, firsts, ov_ref, q)
    for q in range(SPLIT, out_ref.shape[0]):
        out_ref[q] = mix(one, firsts, ov_ref, q - SPLIT + 1)


def flat_spec(shape, count=None):
    lead = tuple(shape[:-1]) if count is None else (count,) + tuple(shape[1:-1])
    return pl.BlockSpec(lead + (BLOCK,), lambda i: (0,) * len(lead) + (i,))


def columnwise(kernel, args, specs, outs, name):
    cells = outs[0][-1]
    return pl.pallas_call(
        kernel,
        grid=(cells // BLOCK,),
        out_shape=[jax.ShapeDtypeStruct(o, jnp.float32) for o in outs],
        in_specs=specs,
        out_specs=[flat_spec(o) for o in outs],
        compiler_params=params(),
        cost_estimate=SMALL,
        name=name,
    )(*args)


def remap_theta(sources, firsts, overlap, log_ratio, surface):
    cells = surface.shape[1]
    args = [*sources, overlap, log_ratio, surface]
    specs = [flat_spec(x.shape, 1) for x in sources]
    specs += [flat_spec(overlap.shape, used(sources)), flat_spec(log_ratio.shape)]
    specs += [flat_spec(surface.shape)]
    level = (LAYERS, cells)
    return columnwise(
        functools.partial(theta_kernel, firsts), args, specs,
        [level, level, (1, cells)], "remap_theta",
    )


def used(sources):
    return sum(x.shape[1] for x in sources)


def remap_tracers(one, two, firsts, overlap, tracers):
    args = [*one, *two]
    specs = [flat_spec(x.shape) for x in args]
    specs += [flat_spec(overlap.shape, used(one))]
    return columnwise(
        functools.partial(tracer_kernel, firsts), [*args, overlap], specs,
        [(tracers, LAYERS, overlap.shape[2])], "remap_tracers",
    )[0]


def on_device(lat_total, tracers, delp, theta, wind_x, wind_y, surface, level_weight):
    count, layers, cells = tracers.shape
    bands, groups = lax.axis_size("lat"), lax.axis_size("lev")
    band, lev = lax.axis_index("lat"), lax.axis_index("lev")
    half = HALF * NLON
    to_south = [(i, i + 1) for i in range(bands - 1)]
    to_north = [(i + 1, i) for i in range(bands - 1)]

    def beside(parts):
        last = jnp.concatenate([p[:, :, half:] for p in parts], axis=0)
        leading = jnp.concatenate([p[:, :, :half] for p in parts], axis=0)
        return lax.ppermute(last, "lat", to_south), lax.ppermute(leading, "lat", to_north)

    first_row = (band * ROWS).astype(jnp.int32)
    row_index = (first_row + jnp.arange(ROWS, dtype=jnp.int32)).astype(jnp.float32)
    latitude = jnp.pi * ((row_index + 0.5) / lat_total - 0.5)
    k = 0.25 * jnp.maximum(0.0, 1.0 - 2.0 * jnp.cos(latitude))
    north, south = beside([delp[None], wind_x[None], wind_y[None]])
    halo_one = beside([theta[None], tracers[SPLIT:]])
    halo_two = beside([tracers[:SPLIT]])
    thick, *rows = prepare(
        first_row[None], k, delp, wind_x, wind_y, north, south, lat_total
    )
    thick_all = lax.all_gather(thick, "lev", axis=0)
    down = lambda by: [(i + by, i) for i in range(groups - by)]
    up = lambda by: [(i, i + by) for i in range(groups - by)]

    def window(first, last):
        return lax.ppermute(last, "lev", up(1)), lax.ppermute(first, "lev", down(1))

    one = transport((count - SPLIT + 1) // 2, SPLIT, theta, k, tracers, *halo_one, *rows)
    near_one = window(*one)
    two = transport(SPLIT // 2, 0, None, k, tracers, *halo_two, *rows)
    near_two = window(*two)
    places = [(0, l) for l in range(LAYERS)]
    places += [(-1, 2), (-1, 3), (1, 0), (1, 1), (-1, 1), (1, 2)]
    overlap, new_delp, log_ratio, choice = edges(
        level_weight, lev[None], thick_all, (False, places)
    )

    def finish(one, two, firsts, overlap, log_ratio, surface):
        new_theta, partial, total = remap_theta(one, firsts, overlap, log_ratio, surface)
        above = sum(lax.ppermute(total, "lev", down(by)) for by in range(1, groups))
        new_tracers = remap_tracers(one, two, firsts, overlap, count)
        return new_tracers, new_theta, partial + above

    def reach_two(one, two, overlap, log_ratio, surface, thick_all):
        return finish(one, two, (0, 2, 4, 6), overlap, log_ratio, surface)

    def reach_three(one, two, overlap, log_ratio, surface, thick_all):
        def more(first, last, *near):
            return (first, last, *near, *window(last[:, :1], first[:, 1:]))

        firsts = (0, 2, 4, 6, 8, 9)
        return finish(more(*one), more(*two), firsts, overlap, log_ratio, surface)

    def reach_all(one, two, overlap, log_ratio, surface, thick_all):
        places = [(-by, l) for by in range(groups) for l in range(LAYERS)]
        overlap = edges(level_weight, lev[None], thick_all, (True, places))[0]

        def around(x):
            turned = [
                lax.ppermute(x, "lev", [(i, (i + by) % groups) for i in range(groups)])
                for by in range(1, groups)
            ]
            return [x, *turned]

        def spread(first, last, *near):
            return (*around(first), *around(last))

        starts = range(0, groups * LAYERS, LAYERS)
        firsts = (*starts, *(i + 2 for i in starts))
        return finish(spread(*one), spread(*two), firsts, overlap, log_ratio, surface)

    new_tracers, new_theta, geopotential = lax.switch(
        choice[0],
        [reach_two, reach_three, reach_all],
        (*one, *near_one), (*two, *near_two), overlap, log_ratio, surface[None], thick_all,
    )
    return new_tracers, new_theta, new_delp, geopotential


def solution(mesh):
    lat_total = ROWS * mesh.shape["lat"]
    return jax.shard_map(
        functools.partial(on_device, lat_total),
        mesh=mesh,
        in_specs=(
            P(None, "lev", "lat"),
            P("lev", "lat"),
            P("lev", "lat"),
            P("lev", "lat"),
            P("lev", "lat"),
            P("lat"),
            P(),
        ),
        out_specs=(P(None, "lev", "lat"), P("lev", "lat"), P("lev", "lat"), P("lev", "lat")),
        check_vma=False,
    )
```

```python
import functools

import jax
import jax.numpy as jnp
from jax import lax
from jax.experimental import pallas as pl
from jax.experimental.pallas import tpu as pltpu
from jax.sharding import PartitionSpec as P

NLON = 2880
WIDE = 2944
HALF = 4
ROWS = 8
LAYERS = 4
BLOCK = 5760
TOP = 1.0
ROW_UNROLL = 4
SMOOTH_UNROLL = 4
PAIR_UNROLL = 2
SPLIT = 4
VMEM_LIMIT = 60 * 1024 * 1024


def params(**extra):
    return pltpu.CompilerParams(vmem_limit_bytes=VMEM_LIMIT, **extra)


SMALL = pl.CostEstimate(flops=1000, bytes_accessed=1000, transcendentals=0)


def shift(x, by):
    return pltpu.roll(x, by % WIDE, 1)


def wrap(x, odd):
    if odd:
        x = shift(x, -64)
    lane = lax.broadcasted_iota(jnp.int32, (8, 128), 1)
    first, last = x[:, :128], x[:, WIDE - 128 :]
    ends = jnp.where(lane < 96, pltpu.roll(first, 64, 1), pltpu.roll(last, 64, 1))
    last = jnp.where(lane < 64, last, ends)
    return jnp.concatenate([x[:, : WIDE - 128], last], axis=1)


def widen(own, north, south, put):
    def pairs(source, count, first):
        def pair(i, carry):
            base = pl.multiple_of(i * (2 * NLON), 128)
            put(first + 2 * i, wrap(source(base), False))
            put(first + 2 * i + 1, wrap(source(base + NLON - 64), True))
            return carry

        lax.fori_loop(0, count, pair, 0, unroll=PAIR_UNROLL)

    pairs(north, HALF // 2, 0)
    pairs(own, ROWS // 2, HALF)
    pairs(south, HALF // 2, HALF + ROWS)


def advance(f_ref, a_ref, b_ref, c_ref, out_ref, count, offset):
    def face(i):
        return a_ref[i + offset] * (
            7.0 * (f_ref[i + 1] + f_ref[i + 2]) - (f_ref[i] + f_ref[i + 3])
        )

    def row(i, carry):
        f = f_ref[i + 2]
        west, east = shift(f, 1), shift(f, -1)
        west_flux = b_ref[i + offset] * (7.0 * (west + f) - (shift(f, 2) + east))
        east_flux = c_ref[i + offset] * (7.0 * (f + east) - (west + shift(f, -2)))
        out_ref[i] = f - (face(i + 1) - face(i)) - (east_flux - west_flux)
        return carry

    lax.fori_loop(0, count, row, 0, unroll=ROW_UNROLL)


def smooth(f_ref, k_ref):
    def row(i, carry):
        k = k_ref[i]
        keep = 1.0 - 2.0 * k
        f = f_ref[i]
        near = shift(f, 1) + shift(f, -1)
        middle = shift(f, 2) + shift(f, -2)
        outer = shift(f, 3) + shift(f, -3)
        f_ref[i] = (
            (keep * keep * keep + 6.0 * keep * k * k) * f
            + (3.0 * keep * keep * k + 3.0 * k * k * k) * near
            + (3.0 * keep * k * k) * middle
            + (k * k * k) * outer
        )
        return carry

    largest = k_ref[0]
    for i in range(1, ROWS):
        largest = jnp.maximum(largest, k_ref[i])

    @pl.when(largest > 0.0)
    def _():
        lax.fori_loop(0, ROWS, row, 0, unroll=SMOOTH_UNROLL)


def emit(f_ref, store, scale_ref=None):
    lane = lax.broadcasted_iota(jnp.int32, (8, 128), 1)

    def pair(i, carry):
        even, odd = f_ref[2 * i], f_ref[2 * i + 1]
        if scale_ref is not None:
            even, odd = even * scale_ref[2 * i], odd * scale_ref[2 * i + 1]
        odd = shift(odd, 64)
        middle = jnp.where(lane < 64, even[:, WIDE - 128 :], odd[:, :128])
        base = pl.multiple_of(i * (2 * NLON), 128)
        store(base, jnp.concatenate([even[:, : WIDE - 128], middle, odd[:, 128:]], axis=1))
        return carry

    lax.fori_loop(0, ROWS // 2, pair, 0, unroll=PAIR_UNROLL)


def both(x):
    return jnp.concatenate([x, x], axis=0)


def prepare_kernel(
    lat_total, row_ref, k_ref, delp_ref, wx_ref, wy_ref, north_ref, south_ref,
    thick_ref, *refs,
):
    def load(ref, field, put):
        widen(
            lambda at: both(ref[:, pl.ds(at, WIDE)]),
            lambda at: both(north_ref[field, :, pl.ds(at, WIDE)]),
            lambda at: both(south_ref[field, :, pl.ds(at, WIDE)]),
            put,
        )

    outs = refs[:5]
    a_ref, b_ref, c_ref, d_ref, r_ref, x_ref, f1_ref, f2_ref, sem = refs[5:]
    held = (a_ref, b_ref, c_ref, d_ref, r_ref)
    copies = [
        pltpu.make_async_copy(held[i], outs[i], sem.at[i]) for i in range(len(outs))
    ]
    first = row_ref[0]

    def put_x(r, x):
        x_ref[r] = x

    def put_d(r, x):
        d_ref[r] = x

    load(wy_ref, 2, put_x)

    def face(i, carry):
        at = first + (i - 2)
        scale = jnp.where((at > 0) & (at < lat_total), 1.0 / 24.0, 0.0)
        a_ref[i] = scale * (x_ref[i + 1] + x_ref[i + 2])
        return carry

    lax.fori_loop(0, 13, face, 0)
    copies[0].start()
    load(wx_ref, 1, put_x)

    def east(i, carry):
        w = x_ref[i + 2]
        b_ref[i] = (1.0 / 24.0) * (shift(w, 1) + w)
        c_ref[i] = (1.0 / 24.0) * (w + shift(w, -1))
        return carry

    lax.fori_loop(0, 12, east, 0, unroll=2)
    copies[1].start()
    copies[2].start()
    load(delp_ref, 0, put_d)
    copies[3].start()
    advance(d_ref, a_ref, b_ref, c_ref, f1_ref, 12, 0)
    advance(f1_ref, a_ref, b_ref, c_ref, f2_ref, 8, 2)
    smooth(f2_ref, k_ref)

    def store(base, x):
        thick_ref[:, pl.ds(base, x.shape[1])] = x[:LAYERS]

    def invert(i, carry):
        r_ref[i] = 1.0 / f2_ref[i]
        return carry

    lax.fori_loop(0, ROWS, invert, 0)
    copies[4].start()
    emit(f2_ref, store)
    for copy in copies:
        copy.wait()


def whole(*shape):
    return pl.BlockSpec(shape, lambda *_: (0,) * len(shape))


def pack_kernel(*refs):
    north_ref, south_ref = refs[-2:]
    half = north_ref.shape[2]
    for i, ref in enumerate(refs[:-2]):
        north_ref[i] = ref[:, :half]
        south_ref[i] = ref[:, half:]


def pack(*fields):
    layers, cells = fields[0].shape
    shape = (len(fields), layers, cells // 2)
    return pl.pallas_call(
        pack_kernel,
        grid=(1,),
        out_shape=[jax.ShapeDtypeStruct(shape, jnp.float32)] * 2,
        in_specs=[whole(layers, cells)] * len(fields),
        out_specs=[whole(*shape)] * 2,
        compiler_params=params(),
        cost_estimate=SMALL,
        name="pack",
    )(*fields)


def prepare(first_row, k, delp, wx, wy, north, south, lat_total):
    rows = (13, 12, 12, 16, 8)
    flat = whole(*delp.shape)
    halo = whole(*north.shape)
    smem = pl.BlockSpec(memory_space=pltpu.SMEM)
    return pl.pallas_call(
        functools.partial(prepare_kernel, lat_total),
        grid=(1,),
        out_shape=[jax.ShapeDtypeStruct(delp.shape, jnp.float32)]
        + [jax.ShapeDtypeStruct((n, 8, WIDE), jnp.float32) for n in rows],
        in_specs=[smem, smem, flat, flat, flat, halo, halo],
        out_specs=[flat] + [pl.BlockSpec(memory_space=pl.ANY)] * len(rows),
        scratch_shapes=[
            pltpu.VMEM((n, 8, WIDE), jnp.float32) for n in (*rows, 16, 12, 8)
        ]
        + [pltpu.SemaphoreType.DMA((len(rows),))],
        compiler_params=params(),
        cost_estimate=SMALL,
        name="prepare",
    )(first_row, k, delp, wx, wy, north, south)


def transport_kernel(with_theta, *refs):
    if with_theta:
        theta_ref, *refs = refs
    (
        k_ref, lower_ref, upper_ref, north_ref, south_ref,
        *sources, first_ref, last_ref, f0_ref, f1_ref, f2_ref,
        a_ref, b_ref, c_ref, d_ref, r_ref, sem,
    ) = refs
    pair = pl.program_id(0)
    held = (a_ref, b_ref, c_ref, d_ref, r_ref)
    copies = [
        pltpu.make_async_copy(sources[i], held[i], sem.at[i]) for i in range(len(held))
    ]

    @pl.when(pair == 0)
    def _():
        for i in (3, 0, 1, 2, 4):
            copies[i].start()
        copies[3].wait()

    def lower(s):
        x = lower_ref[0, :, pl.ds(s, WIDE)]
        if not with_theta:
            return x
        return jnp.where(pair == 0, theta_ref[:, pl.ds(s, WIDE)], x)

    def put(r, x):
        f0_ref[r] = x * d_ref[r]

    widen(
        lambda at: jnp.concatenate([lower(at), upper_ref[0, :, pl.ds(at, WIDE)]], axis=0),
        lambda at: jnp.concatenate(
            [north_ref[0, :, pl.ds(at, WIDE)], north_ref[1, :, pl.ds(at, WIDE)]], axis=0
        ),
        lambda at: jnp.concatenate(
            [south_ref[0, :, pl.ds(at, WIDE)], south_ref[1, :, pl.ds(at, WIDE)]], axis=0
        ),
        put,
    )

    @pl.when(pair == 0)
    def _():
        for i in (0, 1, 2, 4):
            copies[i].wait()

    advance(f0_ref, a_ref, b_ref, c_ref, f1_ref, 12, 0)
    advance(f1_ref, a_ref, b_ref, c_ref, f2_ref, 8, 2)
    smooth(f2_ref, k_ref)

    def store(base, x):
        at = pl.ds(base, x.shape[1])
        for field in range(2):
            first_ref[field, :, at] = x[LAYERS * field : LAYERS * field + 2]
            last_ref[field, :, at] = x[LAYERS * field + 2 : LAYERS * field + 4]

    emit(f2_ref, store, r_ref)


def transport(pairs, first, theta, k, tracers, north, south, *rows):
    cells = tracers.shape[2]
    lead = 0 if theta is None else 1
    field = lambda index: pl.BlockSpec((1, LAYERS, cells), index)
    halo = pl.BlockSpec((2, LAYERS, HALF * NLON), lambda p: (p, 0, 0))
    in_specs = [
        pl.BlockSpec(memory_space=pltpu.SMEM),
        field(lambda p: (jnp.maximum(first + 2 * p - lead, first), 0, 0)),
        field(lambda p: (first + 2 * p + 1 - lead, 0, 0)),
        halo, halo, *[pl.BlockSpec(memory_space=pl.ANY)] * len(rows),
    ]
    args = [k, tracers, tracers, north, south, *rows]
    half = pl.BlockSpec((2, 2, cells), lambda p: (p, 0, 0))
    if lead:
        in_specs = [whole(*theta.shape)] + in_specs
        args = [theta] + args
    return pl.pallas_call(
        functools.partial(transport_kernel, bool(lead)),
        grid=(pairs,),
        out_shape=[jax.ShapeDtypeStruct((2 * pairs, 2, cells), jnp.float32)] * 2,
        in_specs=in_specs,
        out_specs=[half, half],
        scratch_shapes=[
            pltpu.VMEM((n, 8, WIDE), jnp.float32)
            for n in (16, 12, 8, *[x.shape[0] for x in rows])
        ]
        + [pltpu.SemaphoreType.DMA((len(rows),))],
        compiler_params=params(),
        cost_estimate=SMALL,
        name="transport",
    )(*args)


def edges_kernel(
    rows, weight_ref, lev_ref, thick_ref,
    ov_ref, delp_ref, log_ref, choice_ref, edge_ref, flag_ref,
):
    wrapped, places = rows
    groups, _, width = thick_ref.shape
    levels = groups * LAYERS
    lev = lev_ref[0]
    sums = [jnp.float32(0.0)]
    for l in range(levels):
        sums.append(sums[-1] + weight_ref[l])
    edge = jnp.full((1, width), TOP, jnp.float32)
    marks = []
    for l in range(levels):
        edge_ref[l // LAYERS, l % LAYERS : l % LAYERS + 1] = edge
        marks.append(edge)
        edge = edge + thick_ref[l // LAYERS, l % LAYERS : l % LAYERS + 1]
    scale = (edge - TOP) / jnp.full((1, width), sums[levels], jnp.float32)
    level = lax.broadcasted_iota(jnp.int32, (LAYERS, width), 0)
    low = jnp.zeros((LAYERS, width), jnp.float32)
    high = low
    own = [sums[i] for i in range(LAYERS + 1)]
    for g in range(1, groups):
        own = [jnp.where(lev == g, sums[g * LAYERS + i], own[i]) for i in range(LAYERS + 1)]
    for i in range(LAYERS):
        low = jnp.where(level == i, own[i], low)
        high = jnp.where(level == i, own[i + 1], high)
    low, high = TOP + low * scale, TOP + high * scale
    delp = high - low
    delp_ref[...] = delp
    log_ref[...] = jnp.log(high / low)
    inverse = 1.0 / delp
    for i, (away, l) in enumerate(places):
        if wrapped:
            group = lax.rem(lev + away + groups, groups)
        else:
            group = jnp.clip(lev + away, 0, groups - 1)
        base = jnp.broadcast_to(edge_ref[group, l : l + 1], (LAYERS, width))
        limit = jnp.broadcast_to(thick_ref[group, l : l + 1], (LAYERS, width))
        part = jnp.minimum(jnp.maximum(high - base, 0.0), limit) - jnp.minimum(
            jnp.maximum(low - base, 0.0), limit
        )
        ov_ref[i] = part * inverse

    step = pl.program_id(0)

    @pl.when(step == 0)
    def _():
        flag_ref[...] = jnp.full(flag_ref.shape, -1.0, jnp.float32)

    worst = [None, None]
    for m in range(LAYERS, levels, LAYERS):
        target = TOP + sums[m] * scale
        for i in range(2):
            over = jnp.maximum(marks[m - 2 - i] - target, target - marks[m + 2 + i])
            worst[i] = over if worst[i] is None else jnp.maximum(worst[i], over)
    for i in range(2):
        best = worst[i][:, :128]
        for c in range(128, width, 128):
            best = jnp.maximum(best, worst[i][:, c : c + 128])
        flag_ref[i : i + 1] = jnp.maximum(flag_ref[i : i + 1], best)

    @pl.when(step == pl.num_programs(0) - 1)
    def _():
        two, three = jnp.max(flag_ref[0:1]), jnp.max(flag_ref[1:2])
        choice_ref[0] = jnp.where(two <= 0.0, 0, jnp.where(three <= 0.0, 1, 2))


def edges(weight, lev, thick, rows):
    groups, _, cells = thick.shape
    count = len(rows[1])
    smem = pl.BlockSpec(memory_space=pltpu.SMEM)
    own = pl.BlockSpec((LAYERS, BLOCK), lambda i: (0, i))
    level = jax.ShapeDtypeStruct((LAYERS, cells), jnp.float32)
    return pl.pallas_call(
        functools.partial(edges_kernel, rows),
        grid=(cells // BLOCK,),
        out_shape=[
            jax.ShapeDtypeStruct((count, LAYERS, cells), jnp.float32),
            level, level, jax.ShapeDtypeStruct((1,), jnp.int32),
        ],
        in_specs=[smem, smem, pl.BlockSpec((groups, LAYERS, BLOCK), lambda i: (0, 0, i))],
        out_specs=[
            pl.BlockSpec((count, LAYERS, BLOCK), lambda i: (0, 0, i)),
            own, own, smem,
        ],
        scratch_shapes=[
            pltpu.VMEM((groups, LAYERS, BLOCK), jnp.float32),
            pltpu.VMEM((8, 128), jnp.float32),
        ],
        compiler_params=params(),
        cost_estimate=SMALL,
        name="edges",
    )(weight, lev, thick)


def mix(sources, firsts, ov_ref, field):
    width = ov_ref.shape[2]
    total = None
    for density, first in zip(sources, firsts):
        for l in range(density.shape[1]):
            x = jnp.broadcast_to(density[field, l : l + 1], (LAYERS, width))
            term = x * ov_ref[first + l]
            total = term if total is None else total + term
    return total


def theta_kernel(firsts, *refs):
    n = len(firsts)
    ov_ref, log_ref, surface_ref, theta_ref, part_ref, sum_ref = refs[n:]
    theta = mix(refs[:n], firsts, ov_ref, 0)
    theta_ref[...] = theta
    column = theta * log_ref[...]
    partial = jnp.zeros((1, column.shape[1]), jnp.float32)
    for k in range(LAYERS - 1, -1, -1):
        partial = partial + column[k : k + 1]
        part_ref[k : k + 1] = partial + surface_ref[...]
    sum_ref[...] = partial


def tracer_kernel(firsts, *refs):
    n = len(firsts)
    one, two, ov_ref, out_ref = refs[:n], refs[n : 2 * n], refs[-2], refs[-1]
    for q in range(SPLIT):
        out_ref[q] = mix(two, firsts, ov_ref, q)
    for q in range(SPLIT, out_ref.shape[0]):
        out_ref[q] = mix(one, firsts, ov_ref, q - SPLIT + 1)


def flat_spec(shape, count=None):
    lead = tuple(shape[:-1]) if count is None else (count,) + tuple(shape[1:-1])
    return pl.BlockSpec(lead + (BLOCK,), lambda i: (0,) * len(lead) + (i,))


def columnwise(kernel, args, specs, outs, name):
    cells = outs[0][-1]
    return pl.pallas_call(
        kernel,
        grid=(cells // BLOCK,),
        out_shape=[jax.ShapeDtypeStruct(o, jnp.float32) for o in outs],
        in_specs=specs,
        out_specs=[flat_spec(o) for o in outs],
        compiler_params=params(),
        cost_estimate=SMALL,
        name=name,
    )(*args)


def remap_theta(sources, firsts, overlap, log_ratio, surface):
    cells = surface.shape[1]
    args = [*sources, overlap, log_ratio, surface]
    specs = [flat_spec(x.shape, 1) for x in sources]
    specs += [flat_spec(overlap.shape, used(sources)), flat_spec(log_ratio.shape)]
    specs += [flat_spec(surface.shape)]
    level = (LAYERS, cells)
    return columnwise(
        functools.partial(theta_kernel, firsts), args, specs,
        [level, level, (1, cells)], "remap_theta",
    )


def used(sources):
    return sum(x.shape[1] for x in sources)


def remap_tracers(one, two, firsts, overlap, tracers):
    args = [*one, *two]
    specs = [flat_spec(x.shape) for x in args]
    specs += [flat_spec(overlap.shape, used(one))]
    return columnwise(
        functools.partial(tracer_kernel, firsts), [*args, overlap], specs,
        [(tracers, LAYERS, overlap.shape[2])], "remap_tracers",
    )[0]


def on_device(lat_total, tracers, delp, theta, wind_x, wind_y, surface, level_weight):
    count, layers, cells = tracers.shape
    bands, groups = lax.axis_size("lat"), lax.axis_size("lev")
    band, lev = lax.axis_index("lat"), lax.axis_index("lev")
    half = HALF * NLON
    to_south = [(i, i + 1) for i in range(bands - 1)]
    to_north = [(i + 1, i) for i in range(bands - 1)]

    def beside(parts):
        last = jnp.concatenate([p[:, :, half:] for p in parts], axis=0)
        leading = jnp.concatenate([p[:, :, :half] for p in parts], axis=0)
        return exchange(leading, last)

    def exchange(leading, last):
        return lax.ppermute(last, "lat", to_south), lax.ppermute(leading, "lat", to_north)

    first_row = (band * ROWS).astype(jnp.int32)
    row_index = (first_row + jnp.arange(ROWS, dtype=jnp.int32)).astype(jnp.float32)
    latitude = jnp.pi * ((row_index + 0.5) / lat_total - 0.5)
    k = 0.25 * jnp.maximum(0.0, 1.0 - 2.0 * jnp.cos(latitude))
    north, south = exchange(*pack(delp, wind_x, wind_y))
    halo_one = beside([theta[None], tracers[SPLIT:]])
    halo_two = beside([tracers[:SPLIT]])
    thick, *rows = prepare(
        first_row[None], k, delp, wind_x, wind_y, north, south, lat_total
    )
    thick_all = lax.all_gather(thick, "lev", axis=0)
    down = lambda by: [(i + by, i) for i in range(groups - by)]
    up = lambda by: [(i, i + by) for i in range(groups - by)]

    def window(first, last):
        return lax.ppermute(last, "lev", up(1)), lax.ppermute(first, "lev", down(1))

    one = transport((count - SPLIT + 1) // 2, SPLIT, theta, k, tracers, *halo_one, *rows)
    near_one = window(*one)
    two = transport(SPLIT // 2, 0, None, k, tracers, *halo_two, *rows)
    near_two = window(*two)
    places = [(0, l) for l in range(LAYERS)]
    places += [(-1, 2), (-1, 3), (1, 0), (1, 1), (-1, 1), (1, 2)]
    overlap, new_delp, log_ratio, choice = edges(
        level_weight, lev[None], thick_all, (False, places)
    )

    def finish(one, two, firsts, overlap, log_ratio, surface):
        new_theta, partial, total = remap_theta(one, firsts, overlap, log_ratio, surface)
        above = sum(lax.ppermute(total, "lev", down(by)) for by in range(1, groups))
        new_tracers = remap_tracers(one, two, firsts, overlap, count)
        return new_tracers, new_theta, partial + above

    def reach_two(one, two, overlap, log_ratio, surface, thick_all):
        return finish(one, two, (0, 2, 4, 6), overlap, log_ratio, surface)

    def reach_three(one, two, overlap, log_ratio, surface, thick_all):
        def more(first, last, *near):
            return (first, last, *near, *window(last[:, :1], first[:, 1:]))

        firsts = (0, 2, 4, 6, 8, 9)
        return finish(more(*one), more(*two), firsts, overlap, log_ratio, surface)

    def reach_all(one, two, overlap, log_ratio, surface, thick_all):
        places = [(-by, l) for by in range(groups) for l in range(LAYERS)]
        overlap = edges(level_weight, lev[None], thick_all, (True, places))[0]

        def around(x):
            turned = [
                lax.ppermute(x, "lev", [(i, (i + by) % groups) for i in range(groups)])
                for by in range(1, groups)
            ]
            return [x, *turned]

        def spread(first, last, *near):
            return (*around(first), *around(last))

        starts = range(0, groups * LAYERS, LAYERS)
        firsts = (*starts, *(i + 2 for i in starts))
        return finish(spread(*one), spread(*two), firsts, overlap, log_ratio, surface)

    new_tracers, new_theta, geopotential = lax.switch(
        choice[0],
        [reach_two, reach_three, reach_all],
        (*one, *near_one), (*two, *near_two), overlap, log_ratio, surface[None], thick_all,
    )
    return new_tracers, new_theta, new_delp, geopotential


def solution(mesh):
    lat_total = ROWS * mesh.shape["lat"]
    return jax.shard_map(
        functools.partial(on_device, lat_total),
        mesh=mesh,
        in_specs=(
            P(None, "lev", "lat"),
            P("lev", "lat"),
            P("lev", "lat"),
            P("lev", "lat"),
            P("lev", "lat"),
            P("lat"),
            P(),
        ),
        out_specs=(P(None, "lev", "lat"), P("lev", "lat"), P("lev", "lat"), P("lev", "lat")),
        check_vma=False,
    )
```

```python
import functools

import jax
import jax.numpy as jnp
from jax import lax
from jax.experimental import pallas as pl
from jax.experimental.pallas import tpu as pltpu
from jax.sharding import PartitionSpec as P

NLON = 2880
WIDE = 2944
HALF = 4
ROWS = 8
LAYERS = 4
BLOCK = 5760
TOP = 1.0
ROW_UNROLL = 4
COUNTS = (13, 12, 12, 16, 8)
SMOOTH_UNROLL = 4
PAIR_UNROLL = 2
SPLIT = 4
VMEM_LIMIT = 60 * 1024 * 1024
SMALL_LIMIT = 30 * 1024 * 1024


def params(limit=VMEM_LIMIT):
    return pltpu.CompilerParams(vmem_limit_bytes=limit)


SMALL = pl.CostEstimate(flops=1000, bytes_accessed=1000, transcendentals=0)


def shift(x, by):
    return pltpu.roll(x, by % WIDE, 1)


def wrap(x, odd):
    if odd:
        x = shift(x, -64)
    lane = lax.broadcasted_iota(jnp.int32, (8, 128), 1)
    first, last = x[:, :128], x[:, WIDE - 128 :]
    ends = jnp.where(lane < 96, pltpu.roll(first, 64, 1), pltpu.roll(last, 64, 1))
    last = jnp.where(lane < 64, last, ends)
    return jnp.concatenate([x[:, : WIDE - 128], last], axis=1)


def widen(own, north, south, put):
    def pairs(source, count, first):
        def pair(i, carry):
            base = pl.multiple_of(i * (2 * NLON), 128)
            put(first + 2 * i, wrap(source(base), False))
            put(first + 2 * i + 1, wrap(source(base + NLON - 64), True))
            return carry

        lax.fori_loop(0, count, pair, 0, unroll=PAIR_UNROLL)

    pairs(north, HALF // 2, 0)
    pairs(own, ROWS // 2, HALF)
    pairs(south, HALF // 2, HALF + ROWS)


def advance(f_ref, a_ref, b_ref, c_ref, out_ref, count, offset):
    def face(i):
        return a_ref[i + offset] * (
            7.0 * (f_ref[i + 1] + f_ref[i + 2]) - (f_ref[i] + f_ref[i + 3])
        )

    def row(i, carry):
        f = f_ref[i + 2]
        west, east = shift(f, 1), shift(f, -1)
        west_flux = b_ref[i + offset] * (7.0 * (west + f) - (shift(f, 2) + east))
        east_flux = c_ref[i + offset] * (7.0 * (f + east) - (west + shift(f, -2)))
        out_ref[i] = f - (face(i + 1) - face(i)) - (east_flux - west_flux)
        return carry

    lax.fori_loop(0, count, row, 0, unroll=ROW_UNROLL)


def smooth(f_ref, k_ref):
    def row(i, carry):
        k = k_ref[i]
        keep = 1.0 - 2.0 * k
        f = f_ref[i]
        near = shift(f, 1) + shift(f, -1)
        middle = shift(f, 2) + shift(f, -2)
        outer = shift(f, 3) + shift(f, -3)
        f_ref[i] = (
            (keep * keep * keep + 6.0 * keep * k * k) * f
            + (3.0 * keep * keep * k + 3.0 * k * k * k) * near
            + (3.0 * keep * k * k) * middle
            + (k * k * k) * outer
        )
        return carry

    largest = k_ref[0]
    for i in range(1, ROWS):
        largest = jnp.maximum(largest, k_ref[i])

    @pl.when(largest > 0.0)
    def _():
        lax.fori_loop(0, ROWS, row, 0, unroll=SMOOTH_UNROLL)


def emit(f_ref, store, scale_ref=None):
    lane = lax.broadcasted_iota(jnp.int32, (8, 128), 1)

    def pair(i, carry):
        even, odd = f_ref[2 * i], f_ref[2 * i + 1]
        if scale_ref is not None:
            even, odd = even * scale_ref[2 * i], odd * scale_ref[2 * i + 1]
        odd = shift(odd, 64)
        middle = jnp.where(lane < 64, even[:, WIDE - 128 :], odd[:, :128])
        base = pl.multiple_of(i * (2 * NLON), 128)
        store(base, jnp.concatenate([even[:, : WIDE - 128], middle, odd[:, 128:]], axis=1))
        return carry

    lax.fori_loop(0, ROWS // 2, pair, 0, unroll=PAIR_UNROLL)


def both(x):
    return jnp.concatenate([x, x], axis=0)


def prepare_kernel(
    lat_total, row_ref, k_ref, delp_ref, wx_ref, wy_ref, north_ref, south_ref,
    thick_ref, *refs,
):
    def load(ref, field, put):
        widen(
            lambda at: both(ref[:, pl.ds(at, WIDE)]),
            lambda at: both(north_ref[field, :, pl.ds(at, WIDE)]),
            lambda at: both(south_ref[field, :, pl.ds(at, WIDE)]),
            put,
        )

    out_ref, a_ref, b_ref, c_ref, d_ref, r_ref, x_ref, f1_ref, f2_ref, sem = refs
    held = (a_ref, b_ref, c_ref, d_ref, r_ref)
    copies = [
        pltpu.make_async_copy(held[i], out_ref.at[part], sem.at[i])
        for i, part in enumerate(parts_of())
    ]
    first = row_ref[0]

    def put_x(r, x):
        x_ref[r] = x

    def put_d(r, x):
        d_ref[r] = x

    load(wy_ref, 2, put_x)

    def face(i, carry):
        at = first + (i - 2)
        scale = jnp.where((at > 0) & (at < lat_total), 1.0 / 24.0, 0.0)
        a_ref[i] = scale * (x_ref[i + 1] + x_ref[i + 2])
        return carry

    lax.fori_loop(0, 13, face, 0)
    copies[0].start()
    load(wx_ref, 1, put_x)

    def east(i, carry):
        w = x_ref[i + 2]
        b_ref[i] = (1.0 / 24.0) * (shift(w, 1) + w)
        c_ref[i] = (1.0 / 24.0) * (w + shift(w, -1))
        return carry

    lax.fori_loop(0, 12, east, 0, unroll=2)
    copies[1].start()
    copies[2].start()
    load(delp_ref, 0, put_d)
    copies[3].start()
    advance(d_ref, a_ref, b_ref, c_ref, f1_ref, 12, 0)
    advance(f1_ref, a_ref, b_ref, c_ref, f2_ref, 8, 2)
    smooth(f2_ref, k_ref)

    def store(base, x):
        thick_ref[:, pl.ds(base, x.shape[1])] = x[:LAYERS]

    def invert(i, carry):
        r_ref[i] = 1.0 / f2_ref[i]
        return carry

    lax.fori_loop(0, ROWS, invert, 0)
    copies[4].start()
    emit(f2_ref, store)
    for copy in copies:
        copy.wait()


def whole(*shape):
    return pl.BlockSpec(shape, lambda *_: (0,) * len(shape))


def pack_kernel(*refs):
    north_ref, south_ref = refs[-2:]
    half = north_ref.shape[2]
    for i, ref in enumerate(refs[:-2]):
        north_ref[i] = ref[:, :half]
        south_ref[i] = ref[:, half:]


def pack(*fields):
    layers, cells = fields[0].shape
    shape = (len(fields), layers, cells // 2)
    return pl.pallas_call(
        pack_kernel,
        grid=(1,),
        out_shape=[jax.ShapeDtypeStruct(shape, jnp.float32)] * 2,
        in_specs=[whole(layers, cells)] * len(fields),
        out_specs=[whole(*shape)] * 2,
        compiler_params=params(),
        cost_estimate=SMALL,
        name="pack",
    )(*fields)


def parts_of():
    starts = [sum(COUNTS[:i]) for i in range(len(COUNTS))]
    return [pl.ds(start, count) for start, count in zip(starts, COUNTS)]


def prepare(first_row, k, delp, wx, wy, north, south, lat_total):
    flat = whole(*delp.shape)
    halo = whole(*north.shape)
    smem = pl.BlockSpec(memory_space=pltpu.SMEM)
    return pl.pallas_call(
        functools.partial(prepare_kernel, lat_total),
        grid=(1,),
        out_shape=[jax.ShapeDtypeStruct(delp.shape, jnp.float32)]
        + [jax.ShapeDtypeStruct((sum(COUNTS), 8, WIDE), jnp.float32)],
        in_specs=[smem, smem, flat, flat, flat, halo, halo],
        out_specs=[flat, pl.BlockSpec(memory_space=pl.ANY)],
        scratch_shapes=[
            pltpu.VMEM((n, 8, WIDE), jnp.float32) for n in (*COUNTS, 16, 12, 8)
        ]
        + [pltpu.SemaphoreType.DMA((len(COUNTS),))],
        compiler_params=params(),
        cost_estimate=SMALL,
        name="prepare",
    )(first_row, k, delp, wx, wy, north, south)


def transport_kernel(with_theta, *refs):
    if with_theta:
        theta_ref, *refs = refs
    (
        k_ref, lower_ref, upper_ref, north_ref, south_ref,
        rows_ref, first_ref, last_ref, f0_ref, f1_ref, f2_ref,
        a_ref, b_ref, c_ref, d_ref, r_ref, sem,
    ) = refs
    pair = pl.program_id(0)
    held = (a_ref, b_ref, c_ref, d_ref, r_ref)
    copies = [
        pltpu.make_async_copy(rows_ref.at[part], held[i], sem.at[i])
        for i, part in enumerate(parts_of())
    ]

    @pl.when(pair == 0)
    def _():
        for i in (3, 0, 1, 2, 4):
            copies[i].start()
        copies[3].wait()

    def lower(s):
        x = lower_ref[0, :, pl.ds(s, WIDE)]
        if not with_theta:
            return x
        return jnp.where(pair == 0, theta_ref[:, pl.ds(s, WIDE)], x)

    def put(r, x):
        f0_ref[r] = x * d_ref[r]

    widen(
        lambda at: jnp.concatenate([lower(at), upper_ref[0, :, pl.ds(at, WIDE)]], axis=0),
        lambda at: jnp.concatenate(
            [north_ref[0, :, pl.ds(at, WIDE)], north_ref[1, :, pl.ds(at, WIDE)]], axis=0
        ),
        lambda at: jnp.concatenate(
            [south_ref[0, :, pl.ds(at, WIDE)], south_ref[1, :, pl.ds(at, WIDE)]], axis=0
        ),
        put,
    )

    @pl.when(pair == 0)
    def _():
        for i in (0, 1, 2, 4):
            copies[i].wait()

    advance(f0_ref, a_ref, b_ref, c_ref, f1_ref, 12, 0)
    advance(f1_ref, a_ref, b_ref, c_ref, f2_ref, 8, 2)
    smooth(f2_ref, k_ref)

    def store(base, x):
        at = pl.ds(base, x.shape[1])
        for field in range(2):
            first_ref[field, :, at] = x[LAYERS * field : LAYERS * field + 2]
            last_ref[field, :, at] = x[LAYERS * field + 2 : LAYERS * field + 4]

    emit(f2_ref, store, r_ref)


def transport(pairs, first, theta, k, tracers, north, south, rows):
    cells = tracers.shape[2]
    lead = 0 if theta is None else 1
    field = lambda index: pl.BlockSpec((1, LAYERS, cells), index)
    halo = pl.BlockSpec((2, LAYERS, HALF * NLON), lambda p: (p, 0, 0))
    in_specs = [
        pl.BlockSpec(memory_space=pltpu.SMEM),
        field(lambda p: (jnp.maximum(first + 2 * p - lead, first), 0, 0)),
        field(lambda p: (first + 2 * p + 1 - lead, 0, 0)),
        halo, halo, pl.BlockSpec(memory_space=pl.ANY),
    ]
    args = [k, tracers, tracers, north, south, rows]
    half = pl.BlockSpec((2, 2, cells), lambda p: (p, 0, 0))
    if lead:
        in_specs = [whole(*theta.shape)] + in_specs
        args = [theta] + args
    return pl.pallas_call(
        functools.partial(transport_kernel, bool(lead)),
        grid=(pairs,),
        out_shape=[jax.ShapeDtypeStruct((2 * pairs, 2, cells), jnp.float32)] * 2,
        in_specs=in_specs,
        out_specs=[half, half],
        scratch_shapes=[
            pltpu.VMEM((n, 8, WIDE), jnp.float32)
            for n in (16, 12, 8, *COUNTS)
        ]
        + [pltpu.SemaphoreType.DMA((len(COUNTS),))],
        compiler_params=params(SMALL_LIMIT),
        cost_estimate=SMALL,
        name="transport",
    )(*args)


def edges_kernel(
    rows, weight_ref, lev_ref, thick_ref,
    ov_ref, delp_ref, log_ref, choice_ref, edge_ref, flag_ref,
):
    wrapped, places = rows
    groups, _, width = thick_ref.shape
    levels = groups * LAYERS
    lev = lev_ref[0]
    sums = [jnp.float32(0.0)]
    for l in range(levels):
        sums.append(sums[-1] + weight_ref[l])
    edge = jnp.full((1, width), TOP, jnp.float32)
    marks = []
    for l in range(levels):
        edge_ref[l // LAYERS, l % LAYERS : l % LAYERS + 1] = edge
        marks.append(edge)
        edge = edge + thick_ref[l // LAYERS, l % LAYERS : l % LAYERS + 1]
    scale = (edge - TOP) / jnp.full((1, width), sums[levels], jnp.float32)
    level = lax.broadcasted_iota(jnp.int32, (LAYERS, width), 0)
    low = jnp.zeros((LAYERS, width), jnp.float32)
    high = low
    own = [sums[i] for i in range(LAYERS + 1)]
    for g in range(1, groups):
        own = [jnp.where(lev == g, sums[g * LAYERS + i], own[i]) for i in range(LAYERS + 1)]
    for i in range(LAYERS):
        low = jnp.where(level == i, own[i], low)
        high = jnp.where(level == i, own[i + 1], high)
    low, high = TOP + low * scale, TOP + high * scale
    delp = high - low
    delp_ref[...] = delp
    log_ref[...] = jnp.log(high / low)
    inverse = 1.0 / delp
    for i, (away, l) in enumerate(places):
        if wrapped:
            group = lax.rem(lev + away + groups, groups)
        else:
            group = jnp.clip(lev + away, 0, groups - 1)
        base = jnp.broadcast_to(edge_ref[group, l : l + 1], (LAYERS, width))
        limit = jnp.broadcast_to(thick_ref[group, l : l + 1], (LAYERS, width))
        part = jnp.minimum(jnp.maximum(high - base, 0.0), limit) - jnp.minimum(
            jnp.maximum(low - base, 0.0), limit
        )
        ov_ref[i] = part * inverse

    step = pl.program_id(0)

    @pl.when(step == 0)
    def _():
        flag_ref[...] = jnp.full(flag_ref.shape, -1.0, jnp.float32)

    worst = [None, None]
    for m in range(LAYERS, levels, LAYERS):
        target = TOP + sums[m] * scale
        for i in range(2):
            over = jnp.maximum(marks[m - 2 - i] - target, target - marks[m + 2 + i])
            worst[i] = over if worst[i] is None else jnp.maximum(worst[i], over)
    for i in range(2):
        best = worst[i][:, :128]
        for c in range(128, width, 128):
            best = jnp.maximum(best, worst[i][:, c : c + 128])
        flag_ref[i : i + 1] = jnp.maximum(flag_ref[i : i + 1], best)

    @pl.when(step == pl.num_programs(0) - 1)
    def _():
        two, three = jnp.max(flag_ref[0:1]), jnp.max(flag_ref[1:2])
        choice_ref[0] = jnp.where(two <= 0.0, 0, jnp.where(three <= 0.0, 1, 2))


def edges(weight, lev, thick, rows):
    groups, _, cells = thick.shape
    count = len(rows[1])
    smem = pl.BlockSpec(memory_space=pltpu.SMEM)
    own = pl.BlockSpec((LAYERS, BLOCK), lambda i: (0, i))
    level = jax.ShapeDtypeStruct((LAYERS, cells), jnp.float32)
    return pl.pallas_call(
        functools.partial(edges_kernel, rows),
        grid=(cells // BLOCK,),
        out_shape=[
            jax.ShapeDtypeStruct((count, LAYERS, cells), jnp.float32),
            level, level, jax.ShapeDtypeStruct((1,), jnp.int32),
        ],
        in_specs=[smem, smem, pl.BlockSpec((groups, LAYERS, BLOCK), lambda i: (0, 0, i))],
        out_specs=[
            pl.BlockSpec((count, LAYERS, BLOCK), lambda i: (0, 0, i)),
            own, own, smem,
        ],
        scratch_shapes=[
            pltpu.VMEM((groups, LAYERS, BLOCK), jnp.float32),
            pltpu.VMEM((8, 128), jnp.float32),
        ],
        compiler_params=params(),
        cost_estimate=SMALL,
        name="edges",
    )(weight, lev, thick)


def mix(sources, firsts, ov_ref, field):
    width = ov_ref.shape[2]
    total = None
    for density, first in zip(sources, firsts):
        for l in range(density.shape[1]):
            x = jnp.broadcast_to(density[field, l : l + 1], (LAYERS, width))
            term = x * ov_ref[first + l]
            total = term if total is None else total + term
    return total


def theta_kernel(firsts, *refs):
    n = len(firsts)
    ov_ref, log_ref, surface_ref, theta_ref, part_ref, sum_ref = refs[n:]
    theta = mix(refs[:n], firsts, ov_ref, 0)
    theta_ref[...] = theta
    column = theta * log_ref[...]
    partial = jnp.zeros((1, column.shape[1]), jnp.float32)
    for k in range(LAYERS - 1, -1, -1):
        partial = partial + column[k : k + 1]
        part_ref[k : k + 1] = partial + surface_ref[...]
    sum_ref[...] = partial


def tracer_kernel(firsts, *refs):
    n = len(firsts)
    one, two, ov_ref, out_ref = refs[:n], refs[n : 2 * n], refs[-2], refs[-1]
    for q in range(SPLIT):
        out_ref[q] = mix(two, firsts, ov_ref, q)
    for q in range(SPLIT, out_ref.shape[0]):
        out_ref[q] = mix(one, firsts, ov_ref, q - SPLIT + 1)


def flat_spec(shape, count=None):
    lead = tuple(shape[:-1]) if count is None else (count,) + tuple(shape[1:-1])
    return pl.BlockSpec(lead + (BLOCK,), lambda i: (0,) * len(lead) + (i,))


def columnwise(kernel, args, specs, outs, name):
    cells = outs[0][-1]
    return pl.pallas_call(
        kernel,
        grid=(cells // BLOCK,),
        out_shape=[jax.ShapeDtypeStruct(o, jnp.float32) for o in outs],
        in_specs=specs,
        out_specs=[flat_spec(o) for o in outs],
        compiler_params=params(),
        cost_estimate=SMALL,
        name=name,
    )(*args)


def remap_theta(sources, firsts, overlap, log_ratio, surface):
    cells = surface.shape[1]
    args = [*sources, overlap, log_ratio, surface]
    specs = [flat_spec(x.shape, 1) for x in sources]
    specs += [flat_spec(overlap.shape, used(sources)), flat_spec(log_ratio.shape)]
    specs += [flat_spec(surface.shape)]
    level = (LAYERS, cells)
    return columnwise(
        functools.partial(theta_kernel, firsts), args, specs,
        [level, level, (1, cells)], "remap_theta",
    )


def used(sources):
    return sum(x.shape[1] for x in sources)


def remap_tracers(one, two, firsts, overlap, tracers):
    args = [*one, *two]
    specs = [flat_spec(x.shape) for x in args]
    specs += [flat_spec(overlap.shape, used(one))]
    return columnwise(
        functools.partial(tracer_kernel, firsts), [*args, overlap], specs,
        [(tracers, LAYERS, overlap.shape[2])], "remap_tracers",
    )[0]


def on_device(lat_total, tracers, delp, theta, wind_x, wind_y, surface, level_weight):
    count, layers, cells = tracers.shape
    bands, groups = lax.axis_size("lat"), lax.axis_size("lev")
    band, lev = lax.axis_index("lat"), lax.axis_index("lev")
    half = HALF * NLON
    to_south = [(i, i + 1) for i in range(bands - 1)]
    to_north = [(i + 1, i) for i in range(bands - 1)]

    def beside(parts):
        last = jnp.concatenate([p[:, :, half:] for p in parts], axis=0)
        leading = jnp.concatenate([p[:, :, :half] for p in parts], axis=0)
        return exchange(leading, last)

    def exchange(leading, last):
        return lax.ppermute(last, "lat", to_south), lax.ppermute(leading, "lat", to_north)

    first_row = (band * ROWS).astype(jnp.int32)
    row_index = (first_row + jnp.arange(ROWS, dtype=jnp.int32)).astype(jnp.float32)
    latitude = jnp.pi * ((row_index + 0.5) / lat_total - 0.5)
    k = 0.25 * jnp.maximum(0.0, 1.0 - 2.0 * jnp.cos(latitude))
    north, south = exchange(*pack(delp, wind_x, wind_y))
    halo_one = beside([theta[None], tracers[SPLIT:]])
    halo_two = beside([tracers[:SPLIT]])
    thick, rows = prepare(
        first_row[None], k, delp, wind_x, wind_y, north, south, lat_total
    )
    thick_all = lax.all_gather(thick, "lev", axis=0)
    down = lambda by: [(i + by, i) for i in range(groups - by)]
    up = lambda by: [(i, i + by) for i in range(groups - by)]

    def window(first, last):
        return lax.ppermute(last, "lev", up(1)), lax.ppermute(first, "lev", down(1))

    one = transport((count - SPLIT + 1) // 2, SPLIT, theta, k, tracers, *halo_one, rows)
    near_one = window(*one)
    two = transport(SPLIT // 2, 0, None, k, tracers, *halo_two, rows)
    near_two = window(*two)
    places = [(0, l) for l in range(LAYERS)]
    places += [(-1, 2), (-1, 3), (1, 0), (1, 1), (-1, 1), (1, 2)]
    overlap, new_delp, log_ratio, choice = edges(
        level_weight, lev[None], thick_all, (False, places)
    )

    def finish(one, two, firsts, overlap, log_ratio, surface):
        new_theta, partial, total = remap_theta(one, firsts, overlap, log_ratio, surface)
        above = sum(lax.ppermute(total, "lev", down(by)) for by in range(1, groups))
        new_tracers = remap_tracers(one, two, firsts, overlap, count)
        return new_tracers, new_theta, partial + above

    def reach_two(one, two, overlap, log_ratio, surface, thick_all):
        return finish(one, two, (0, 2, 4, 6), overlap, log_ratio, surface)

    def reach_three(one, two, overlap, log_ratio, surface, thick_all):
        def more(first, last, *near):
            return (first, last, *near, *window(last[:, :1], first[:, 1:]))

        firsts = (0, 2, 4, 6, 8, 9)
        return finish(more(*one), more(*two), firsts, overlap, log_ratio, surface)

    def reach_all(one, two, overlap, log_ratio, surface, thick_all):
        places = [(-by, l) for by in range(groups) for l in range(LAYERS)]
        overlap = edges(level_weight, lev[None], thick_all, (True, places))[0]

        def around(x):
            turned = [
                lax.ppermute(x, "lev", [(i, (i + by) % groups) for i in range(groups)])
                for by in range(1, groups)
            ]
            return [x, *turned]

        def spread(first, last, *near):
            return (*around(first), *around(last))

        starts = range(0, groups * LAYERS, LAYERS)
        firsts = (*starts, *(i + 2 for i in starts))
        return finish(spread(*one), spread(*two), firsts, overlap, log_ratio, surface)

    new_tracers, new_theta, geopotential = lax.switch(
        choice[0],
        [reach_two, reach_three, reach_all],
        (*one, *near_one), (*two, *near_two), overlap, log_ratio, surface[None], thick_all,
    )
    return new_tracers, new_theta, new_delp, geopotential


def solution(mesh):
    lat_total = ROWS * mesh.shape["lat"]
    return jax.shard_map(
        functools.partial(on_device, lat_total),
        mesh=mesh,
        in_specs=(
            P(None, "lev", "lat"),
            P("lev", "lat"),
            P("lev", "lat"),
            P("lev", "lat"),
            P("lev", "lat"),
            P("lat"),
            P(),
        ),
        out_specs=(P(None, "lev", "lat"), P("lev", "lat"), P("lev", "lat"), P("lev", "lat")),
        check_vma=False,
    )
```

```python
import functools

import jax
import jax.numpy as jnp
from jax import lax
from jax.experimental import pallas as pl
from jax.experimental.pallas import tpu as pltpu
from jax.sharding import PartitionSpec as P

NLON = 2880
WIDE = 2944
HALF = 4
ROWS = 8
LAYERS = 4
BLOCK = 5760
TOP = 1.0
ROW_UNROLL = 4
COUNTS = (13, 12, 12, 16, 8)
SMOOTH_UNROLL = 4
SPLIT = 4
VMEM_LIMIT = 60 * 1024 * 1024
SMALL_LIMIT = 30 * 1024 * 1024


def params(limit=VMEM_LIMIT):
    return pltpu.CompilerParams(vmem_limit_bytes=limit)


SMALL = pl.CostEstimate(flops=1000, bytes_accessed=1000, transcendentals=0)


def shift(x, by):
    return pltpu.roll(x, by % WIDE, 1)


def wrap(x, odd):
    if odd:
        x = shift(x, -64)
    lane = lax.broadcasted_iota(jnp.int32, (8, 128), 1)
    first, last = x[:, :128], x[:, WIDE - 128 :]
    ends = jnp.where(lane < 96, pltpu.roll(first, 64, 1), pltpu.roll(last, 64, 1))
    last = jnp.where(lane < 64, last, ends)
    return jnp.concatenate([x[:, : WIDE - 128], last], axis=1)


def widen(own, north, south, put):
    def pairs(source, count, first):
        def pair(i, carry):
            base = pl.multiple_of(i * (2 * NLON), 128)
            put(first + 2 * i, wrap(source(base), False))
            put(first + 2 * i + 1, wrap(source(base + NLON - 64), True))
            return carry

        lax.fori_loop(0, count, pair, 0, unroll=count)

    pairs(north, HALF // 2, 0)
    pairs(own, ROWS // 2, HALF)
    pairs(south, HALF // 2, HALF + ROWS)


def advance(f_ref, a_ref, b_ref, c_ref, out_ref, count, offset):
    def face(i):
        return a_ref[i + offset] * (
            7.0 * (f_ref[i + 1] + f_ref[i + 2]) - (f_ref[i] + f_ref[i + 3])
        )

    def row(i, carry):
        f = f_ref[i + 2]
        west, east = shift(f, 1), shift(f, -1)
        west_flux = b_ref[i + offset] * (7.0 * (west + f) - (shift(f, 2) + east))
        east_flux = c_ref[i + offset] * (7.0 * (f + east) - (west + shift(f, -2)))
        out_ref[i] = f - (face(i + 1) - face(i)) - (east_flux - west_flux)
        return carry

    lax.fori_loop(0, count, row, 0, unroll=ROW_UNROLL)


def smooth(f_ref, k_ref):
    def row(i, carry):
        k = k_ref[i]
        keep = 1.0 - 2.0 * k
        f = f_ref[i]
        near = shift(f, 1) + shift(f, -1)
        middle = shift(f, 2) + shift(f, -2)
        outer = shift(f, 3) + shift(f, -3)
        f_ref[i] = (
            (keep * keep * keep + 6.0 * keep * k * k) * f
            + (3.0 * keep * keep * k + 3.0 * k * k * k) * near
            + (3.0 * keep * k * k) * middle
            + (k * k * k) * outer
        )
        return carry

    largest = k_ref[0]
    for i in range(1, ROWS):
        largest = jnp.maximum(largest, k_ref[i])

    @pl.when(largest > 0.0)
    def _():
        lax.fori_loop(0, ROWS, row, 0, unroll=SMOOTH_UNROLL)


def emit(f_ref, store, scale_ref=None):
    lane = lax.broadcasted_iota(jnp.int32, (8, 128), 1)

    def pair(i, carry):
        even, odd = f_ref[2 * i], f_ref[2 * i + 1]
        if scale_ref is not None:
            even, odd = even * scale_ref[2 * i], odd * scale_ref[2 * i + 1]
        odd = shift(odd, 64)
        middle = jnp.where(lane < 64, even[:, WIDE - 128 :], odd[:, :128])
        base = pl.multiple_of(i * (2 * NLON), 128)
        store(base, jnp.concatenate([even[:, : WIDE - 128], middle, odd[:, 128:]], axis=1))
        return carry

    lax.fori_loop(0, ROWS // 2, pair, 0, unroll=4)


def both(x):
    return jnp.concatenate([x, x], axis=0)


def prepare_kernel(
    lat_total, row_ref, k_ref, delp_ref, wx_ref, wy_ref, north_ref, south_ref,
    thick_ref, *refs,
):
    def load(ref, before, after, put):
        widen(
            lambda at: both(ref[:, pl.ds(at, WIDE)]),
            lambda at: both(north_ref[:, pl.ds(at + before, WIDE)]),
            lambda at: both(south_ref[:, pl.ds(at + after, WIDE)]),
            put,
        )

    half, pair = HALF * NLON, 2 * NLON
    out_ref, a_ref, b_ref, c_ref, d_ref, r_ref, x_ref, f1_ref, f2_ref, sem = refs
    held = (a_ref, b_ref, c_ref, d_ref, r_ref)
    copies = [
        pltpu.make_async_copy(held[i], out_ref.at[part], sem.at[i])
        for i, part in enumerate(parts_of())
    ]
    first = row_ref[0]

    def put_x(r, x):
        x_ref[r] = x

    def put_d(r, x):
        d_ref[r] = x

    load(wy_ref, half + pair, half + pair, put_x)

    def face(i, carry):
        at = first + (i - 2)
        scale = jnp.where((at > 0) & (at < lat_total), 1.0 / 24.0, 0.0)
        a_ref[i] = scale * (x_ref[i + 1] + x_ref[i + 2])
        return carry

    lax.fori_loop(0, 13, face, 0)
    copies[0].start()
    load(wx_ref, half - pair, half, put_x)

    def east(i, carry):
        w = x_ref[i + 2]
        b_ref[i] = (1.0 / 24.0) * (shift(w, 1) + w)
        c_ref[i] = (1.0 / 24.0) * (w + shift(w, -1))
        return carry

    lax.fori_loop(0, 12, east, 0, unroll=2)
    copies[1].start()
    copies[2].start()
    load(delp_ref, 0, 0, put_d)
    copies[3].start()
    advance(d_ref, a_ref, b_ref, c_ref, f1_ref, 12, 0)
    advance(f1_ref, a_ref, b_ref, c_ref, f2_ref, 8, 2)
    smooth(f2_ref, k_ref)

    def store(base, x):
        thick_ref[:, pl.ds(base, x.shape[1])] = x[:LAYERS]

    def invert(i, carry):
        r_ref[i] = 1.0 / f2_ref[i]
        return carry

    lax.fori_loop(0, ROWS, invert, 0)
    copies[4].start()
    emit(f2_ref, store)
    for copy in copies:
        copy.wait()


def whole(*shape):
    return pl.BlockSpec(shape, lambda *_: (0,) * len(shape))


def pack_kernel(delp_ref, wx_ref, wy_ref, north_ref, south_ref):
    half, pair = HALF * NLON, 2 * NLON
    cells = delp_ref.shape[1]
    north_ref[:, :half] = delp_ref[:, :half]
    north_ref[:, half : half + pair] = wx_ref[:, :pair]
    north_ref[:, half + pair :] = wy_ref[:, :half]
    south_ref[:, :half] = delp_ref[:, half:]
    south_ref[:, half : half + pair] = wx_ref[:, cells - pair :]
    south_ref[:, half + pair :] = wy_ref[:, half:]


def pack(delp, wx, wy):
    layers, cells = delp.shape
    shape = (layers, (2 * HALF + 2) * NLON)
    return pl.pallas_call(
        pack_kernel,
        grid=(1,),
        out_shape=[jax.ShapeDtypeStruct(shape, jnp.float32)] * 2,
        in_specs=[whole(layers, cells)] * 3,
        out_specs=[whole(*shape)] * 2,
        compiler_params=params(),
        cost_estimate=SMALL,
        name="pack",
    )(delp, wx, wy)


def parts_of():
    starts = [sum(COUNTS[:i]) for i in range(len(COUNTS))]
    return [pl.ds(start, count) for start, count in zip(starts, COUNTS)]


def prepare(first_row, k, delp, wx, wy, north, south, lat_total):
    flat = whole(*delp.shape)
    halo = whole(*north.shape)
    smem = pl.BlockSpec(memory_space=pltpu.SMEM)
    return pl.pallas_call(
        functools.partial(prepare_kernel, lat_total),
        grid=(1,),
        out_shape=[jax.ShapeDtypeStruct(delp.shape, jnp.float32)]
        + [jax.ShapeDtypeStruct((sum(COUNTS), 8, WIDE), jnp.float32)],
        in_specs=[smem, smem, flat, flat, flat, halo, halo],
        out_specs=[flat, pl.BlockSpec(memory_space=pl.ANY)],
        scratch_shapes=[
            pltpu.VMEM((n, 8, WIDE), jnp.float32) for n in (*COUNTS, 16, 12, 8)
        ]
        + [pltpu.SemaphoreType.DMA((len(COUNTS),))],
        compiler_params=params(),
        cost_estimate=SMALL,
        name="prepare",
    )(first_row, k, delp, wx, wy, north, south)


def transport_kernel(with_theta, *refs):
    if with_theta:
        theta_ref, *refs = refs
    (
        k_ref, lower_ref, upper_ref, north_ref, south_ref,
        rows_ref, first_ref, last_ref, f0_ref, f1_ref, f2_ref,
        a_ref, b_ref, c_ref, d_ref, r_ref, sem,
    ) = refs
    pair = pl.program_id(0)
    held = (a_ref, b_ref, c_ref, d_ref, r_ref)
    copies = [
        pltpu.make_async_copy(rows_ref.at[part], held[i], sem.at[i])
        for i, part in enumerate(parts_of())
    ]

    @pl.when(pair == 0)
    def _():
        for i in (3, 0, 1, 2, 4):
            copies[i].start()
        copies[3].wait()

    def lower(s):
        x = lower_ref[0, :, pl.ds(s, WIDE)]
        if not with_theta:
            return x
        return jnp.where(pair == 0, theta_ref[:, pl.ds(s, WIDE)], x)

    def put(r, x):
        f0_ref[r] = x * d_ref[r]

    widen(
        lambda at: jnp.concatenate([lower(at), upper_ref[0, :, pl.ds(at, WIDE)]], axis=0),
        lambda at: jnp.concatenate(
            [north_ref[0, :, pl.ds(at, WIDE)], north_ref[1, :, pl.ds(at, WIDE)]], axis=0
        ),
        lambda at: jnp.concatenate(
            [south_ref[0, :, pl.ds(at, WIDE)], south_ref[1, :, pl.ds(at, WIDE)]], axis=0
        ),
        put,
    )

    @pl.when(pair == 0)
    def _():
        for i in (0, 1, 2, 4):
            copies[i].wait()

    advance(f0_ref, a_ref, b_ref, c_ref, f1_ref, 12, 0)
    advance(f1_ref, a_ref, b_ref, c_ref, f2_ref, 8, 2)
    smooth(f2_ref, k_ref)

    def store(base, x):
        at = pl.ds(base, x.shape[1])
        for field in range(2):
            first_ref[field, :, at] = x[LAYERS * field : LAYERS * field + 2]
            last_ref[field, :, at] = x[LAYERS * field + 2 : LAYERS * field + 4]

    emit(f2_ref, store, r_ref)


def transport(pairs, first, theta, k, tracers, north, south, rows):
    cells = tracers.shape[2]
    lead = 0 if theta is None else 1
    field = lambda index: pl.BlockSpec((1, LAYERS, cells), index)
    halo = pl.BlockSpec((2, LAYERS, HALF * NLON), lambda p: (p, 0, 0))
    in_specs = [
        pl.BlockSpec(memory_space=pltpu.SMEM),
        field(lambda p: (jnp.maximum(first + 2 * p - lead, first), 0, 0)),
        field(lambda p: (first + 2 * p + 1 - lead, 0, 0)),
        halo, halo, pl.BlockSpec(memory_space=pl.ANY),
    ]
    args = [k, tracers, tracers, north, south, rows]
    half = pl.BlockSpec((2, 2, cells), lambda p: (p, 0, 0))
    if lead:
        in_specs = [whole(*theta.shape)] + in_specs
        args = [theta] + args
    return pl.pallas_call(
        functools.partial(transport_kernel, bool(lead)),
        grid=(pairs,),
        out_shape=[jax.ShapeDtypeStruct((2 * pairs, 2, cells), jnp.float32)] * 2,
        in_specs=in_specs,
        out_specs=[half, half],
        scratch_shapes=[
            pltpu.VMEM((n, 8, WIDE), jnp.float32)
            for n in (16, 12, 8, *COUNTS)
        ]
        + [pltpu.SemaphoreType.DMA((len(COUNTS),))],
        compiler_params=params(SMALL_LIMIT),
        cost_estimate=SMALL,
        name="transport",
    )(*args)


def edges_kernel(
    rows, weight_ref, lev_ref, thick_ref,
    ov_ref, delp_ref, log_ref, choice_ref, edge_ref, flag_ref,
):
    wrapped, places = rows
    groups, _, width = thick_ref.shape
    levels = groups * LAYERS
    lev = lev_ref[0]
    sums = [jnp.float32(0.0)]
    for l in range(levels):
        sums.append(sums[-1] + weight_ref[l])
    edge = jnp.full((1, width), TOP, jnp.float32)
    marks = []
    for l in range(levels):
        edge_ref[l // LAYERS, l % LAYERS : l % LAYERS + 1] = edge
        marks.append(edge)
        edge = edge + thick_ref[l // LAYERS, l % LAYERS : l % LAYERS + 1]
    scale = (edge - TOP) / jnp.full((1, width), sums[levels], jnp.float32)
    level = lax.broadcasted_iota(jnp.int32, (LAYERS, width), 0)
    low = jnp.zeros((LAYERS, width), jnp.float32)
    high = low
    own = [sums[i] for i in range(LAYERS + 1)]
    for g in range(1, groups):
        own = [jnp.where(lev == g, sums[g * LAYERS + i], own[i]) for i in range(LAYERS + 1)]
    for i in range(LAYERS):
        low = jnp.where(level == i, own[i], low)
        high = jnp.where(level == i, own[i + 1], high)
    low, high = TOP + low * scale, TOP + high * scale
    delp = high - low
    delp_ref[...] = delp
    log_ref[...] = jnp.log(high / low)
    inverse = 1.0 / delp
    for i, (away, l) in enumerate(places):
        if wrapped:
            group = lax.rem(lev + away + groups, groups)
        else:
            group = jnp.clip(lev + away, 0, groups - 1)
        base = jnp.broadcast_to(edge_ref[group, l : l + 1], (LAYERS, width))
        limit = jnp.broadcast_to(thick_ref[group, l : l + 1], (LAYERS, width))
        part = jnp.minimum(jnp.maximum(high - base, 0.0), limit) - jnp.minimum(
            jnp.maximum(low - base, 0.0), limit
        )
        ov_ref[i] = part * inverse

    step = pl.program_id(0)

    @pl.when(step == 0)
    def _():
        flag_ref[...] = jnp.full(flag_ref.shape, -1.0, jnp.float32)

    worst = [None, None]
    for m in range(LAYERS, levels, LAYERS):
        target = TOP + sums[m] * scale
        for i in range(2):
            over = jnp.maximum(marks[m - 2 - i] - target, target - marks[m + 2 + i])
            worst[i] = over if worst[i] is None else jnp.maximum(worst[i], over)
    for i in range(2):
        best = worst[i][:, :128]
        for c in range(128, width, 128):
            best = jnp.maximum(best, worst[i][:, c : c + 128])
        flag_ref[i : i + 1] = jnp.maximum(flag_ref[i : i + 1], best)

    @pl.when(step == pl.num_programs(0) - 1)
    def _():
        two, three = jnp.max(flag_ref[0:1]), jnp.max(flag_ref[1:2])
        choice_ref[0] = jnp.where(two <= 0.0, 0, jnp.where(three <= 0.0, 1, 2))


def edges(weight, lev, thick, rows):
    groups, _, cells = thick.shape
    count = len(rows[1])
    smem = pl.BlockSpec(memory_space=pltpu.SMEM)
    own = pl.BlockSpec((LAYERS, BLOCK), lambda i: (0, i))
    level = jax.ShapeDtypeStruct((LAYERS, cells), jnp.float32)
    return pl.pallas_call(
        functools.partial(edges_kernel, rows),
        grid=(cells // BLOCK,),
        out_shape=[
            jax.ShapeDtypeStruct((count, LAYERS, cells), jnp.float32),
            level, level, jax.ShapeDtypeStruct((1,), jnp.int32),
        ],
        in_specs=[smem, smem, pl.BlockSpec((groups, LAYERS, BLOCK), lambda i: (0, 0, i))],
        out_specs=[
            pl.BlockSpec((count, LAYERS, BLOCK), lambda i: (0, 0, i)),
            own, own, smem,
        ],
        scratch_shapes=[
            pltpu.VMEM((groups, LAYERS, BLOCK), jnp.float32),
            pltpu.VMEM((8, 128), jnp.float32),
        ],
        compiler_params=params(),
        cost_estimate=SMALL,
        name="edges",
    )(weight, lev, thick)


def mix(sources, firsts, ov_ref, field):
    width = ov_ref.shape[2]
    total = None
    for density, first in zip(sources, firsts):
        for l in range(density.shape[1]):
            x = jnp.broadcast_to(density[field, l : l + 1], (LAYERS, width))
            term = x * ov_ref[first + l]
            total = term if total is None else total + term
    return total


def theta_kernel(firsts, *refs):
    n = len(firsts)
    ov_ref, log_ref, surface_ref, theta_ref, part_ref, sum_ref = refs[n:]
    theta = mix(refs[:n], firsts, ov_ref, 0)
    theta_ref[...] = theta
    column = theta * log_ref[...]
    partial = jnp.zeros((1, column.shape[1]), jnp.float32)
    for k in range(LAYERS - 1, -1, -1):
        partial = partial + column[k : k + 1]
        part_ref[k : k + 1] = partial + surface_ref[...]
    sum_ref[...] = partial


def tracer_kernel(firsts, *refs):
    n = len(firsts)
    one, two, ov_ref, out_ref = refs[:n], refs[n : 2 * n], refs[-2], refs[-1]
    for q in range(SPLIT):
        out_ref[q] = mix(two, firsts, ov_ref, q)
    for q in range(SPLIT, out_ref.shape[0]):
        out_ref[q] = mix(one, firsts, ov_ref, q - SPLIT + 1)


def flat_spec(shape, count=None):
    lead = tuple(shape[:-1]) if count is None else (count,) + tuple(shape[1:-1])
    return pl.BlockSpec(lead + (BLOCK,), lambda i: (0,) * len(lead) + (i,))


def columnwise(kernel, args, specs, outs, name):
    cells = outs[0][-1]
    return pl.pallas_call(
        kernel,
        grid=(cells // BLOCK,),
        out_shape=[jax.ShapeDtypeStruct(o, jnp.float32) for o in outs],
        in_specs=specs,
        out_specs=[flat_spec(o) for o in outs],
        compiler_params=params(),
        cost_estimate=SMALL,
        name=name,
    )(*args)


def remap_theta(sources, firsts, overlap, log_ratio, surface):
    cells = surface.shape[1]
    args = [*sources, overlap, log_ratio, surface]
    specs = [flat_spec(x.shape, 1) for x in sources]
    specs += [flat_spec(overlap.shape, used(sources)), flat_spec(log_ratio.shape)]
    specs += [flat_spec(surface.shape)]
    level = (LAYERS, cells)
    return columnwise(
        functools.partial(theta_kernel, firsts), args, specs,
        [level, level, (1, cells)], "remap_theta",
    )


def used(sources):
    return sum(x.shape[1] for x in sources)


def remap_tracers(one, two, firsts, overlap, tracers):
    args = [*one, *two]
    specs = [flat_spec(x.shape) for x in args]
    specs += [flat_spec(overlap.shape, used(one))]
    return columnwise(
        functools.partial(tracer_kernel, firsts), [*args, overlap], specs,
        [(tracers, LAYERS, overlap.shape[2])], "remap_tracers",
    )[0]


def on_device(lat_total, tracers, delp, theta, wind_x, wind_y, surface, level_weight):
    count, layers, cells = tracers.shape
    bands, groups = lax.axis_size("lat"), lax.axis_size("lev")
    band, lev = lax.axis_index("lat"), lax.axis_index("lev")
    half = HALF * NLON
    to_south = [(i, i + 1) for i in range(bands - 1)]
    to_north = [(i + 1, i) for i in range(bands - 1)]

    def beside(parts):
        last = jnp.concatenate([p[:, :, half:] for p in parts], axis=0)
        leading = jnp.concatenate([p[:, :, :half] for p in parts], axis=0)
        return exchange(leading, last)

    def exchange(leading, last):
        return lax.ppermute(last, "lat", to_south), lax.ppermute(leading, "lat", to_north)

    first_row = (band * ROWS).astype(jnp.int32)
    row_index = (first_row + jnp.arange(ROWS, dtype=jnp.int32)).astype(jnp.float32)
    latitude = jnp.pi * ((row_index + 0.5) / lat_total - 0.5)
    k = 0.25 * jnp.maximum(0.0, 1.0 - 2.0 * jnp.cos(latitude))
    north, south = exchange(*pack(delp, wind_x, wind_y))
    halo_one = beside([theta[None], tracers[SPLIT:]])
    halo_two = beside([tracers[:SPLIT]])
    thick, rows = prepare(
        first_row[None], k, delp, wind_x, wind_y, north, south, lat_total
    )
    thick_all = lax.all_gather(thick, "lev", axis=0)
    down = lambda by: [(i + by, i) for i in range(groups - by)]
    up = lambda by: [(i, i + by) for i in range(groups - by)]

    def window(first, last):
        return lax.ppermute(last, "lev", up(1)), lax.ppermute(first, "lev", down(1))

    one = transport((count - SPLIT + 1) // 2, SPLIT, theta, k, tracers, *halo_one, rows)
    near_one = window(*one)
    two = transport(SPLIT // 2, 0, None, k, tracers, *halo_two, rows)
    near_two = window(*two)
    places = [(0, l) for l in range(LAYERS)]
    places += [(-1, 2), (-1, 3), (1, 0), (1, 1), (-1, 1), (1, 2)]
    overlap, new_delp, log_ratio, choice = edges(
        level_weight, lev[None], thick_all, (False, places)
    )

    def finish(one, two, firsts, overlap, log_ratio, surface):
        new_theta, partial, total = remap_theta(one, firsts, overlap, log_ratio, surface)
        above = sum(lax.ppermute(total, "lev", down(by)) for by in range(1, groups))
        new_tracers = remap_tracers(one, two, firsts, overlap, count)
        return new_tracers, new_theta, partial + above

    def reach_two(one, two, overlap, log_ratio, surface, thick_all):
        return finish(one, two, (0, 2, 4, 6), overlap, log_ratio, surface)

    def reach_three(one, two, overlap, log_ratio, surface, thick_all):
        def more(first, last, *near):
            return (first, last, *near, *window(last[:, :1], first[:, 1:]))

        firsts = (0, 2, 4, 6, 8, 9)
        return finish(more(*one), more(*two), firsts, overlap, log_ratio, surface)

    def reach_all(one, two, overlap, log_ratio, surface, thick_all):
        places = [(-by, l) for by in range(groups) for l in range(LAYERS)]
        overlap = edges(level_weight, lev[None], thick_all, (True, places))[0]

        def around(x):
            turned = [
                lax.ppermute(x, "lev", [(i, (i + by) % groups) for i in range(groups)])
                for by in range(1, groups)
            ]
            return [x, *turned]

        def spread(first, last, *near):
            return (*around(first), *around(last))

        starts = range(0, groups * LAYERS, LAYERS)
        firsts = (*starts, *(i + 2 for i in starts))
        return finish(spread(*one), spread(*two), firsts, overlap, log_ratio, surface)

    new_tracers, new_theta, geopotential = lax.switch(
        choice[0],
        [reach_two, reach_three, reach_all],
        (*one, *near_one), (*two, *near_two), overlap, log_ratio, surface[None], thick_all,
    )
    return new_tracers, new_theta, new_delp, geopotential


def solution(mesh):
    lat_total = ROWS * mesh.shape["lat"]
    return jax.shard_map(
        functools.partial(on_device, lat_total),
        mesh=mesh,
        in_specs=(
            P(None, "lev", "lat"),
            P("lev", "lat"),
            P("lev", "lat"),
            P("lev", "lat"),
            P("lev", "lat"),
            P("lat"),
            P(),
        ),
        out_specs=(P(None, "lev", "lat"), P("lev", "lat"), P("lev", "lat"), P("lev", "lat")),
        check_vma=False,
    )
```

```python
import functools

import jax
import jax.numpy as jnp
from jax import lax
from jax.experimental import pallas as pl
from jax.experimental.pallas import tpu as pltpu
from jax.sharding import PartitionSpec as P

NLON = 2880
WIDE = 2944
HALF = 4
ROWS = 8
LAYERS = 4
BLOCK = 5760
TOP = 1.0
ROW_UNROLL = 4
COUNTS = (13, 12, 12, 16, 8)
SMOOTH_UNROLL = 8
SPLIT = 4
VMEM_LIMIT = 60 * 1024 * 1024
SMALL_LIMIT = 30 * 1024 * 1024


def params(limit=VMEM_LIMIT):
    return pltpu.CompilerParams(vmem_limit_bytes=limit)


SMALL = pl.CostEstimate(flops=1000, bytes_accessed=1000, transcendentals=0)


def shift(x, by):
    return pltpu.roll(x, by % WIDE, 1)


def wrap(x, odd):
    if odd:
        x = shift(x, -64)
    lane = lax.broadcasted_iota(jnp.int32, (8, 128), 1)
    first, last = x[:, :128], x[:, WIDE - 128 :]
    ends = jnp.where(lane < 96, pltpu.roll(first, 64, 1), pltpu.roll(last, 64, 1))
    last = jnp.where(lane < 64, last, ends)
    return jnp.concatenate([x[:, : WIDE - 128], last], axis=1)


def widen(own, north, south, put):
    def pairs(source, count, first):
        def pair(i, carry):
            base = pl.multiple_of(i * (2 * NLON), 128)
            put(first + 2 * i, wrap(source(base), False))
            put(first + 2 * i + 1, wrap(source(base + NLON - 64), True))
            return carry

        lax.fori_loop(0, count, pair, 0, unroll=count)

    pairs(north, HALF // 2, 0)
    pairs(own, ROWS // 2, HALF)
    pairs(south, HALF // 2, HALF + ROWS)


def advance(f_ref, a_ref, b_ref, c_ref, out_ref, count, offset):
    def face(i):
        return a_ref[i + offset] * (
            7.0 * (f_ref[i + 1] + f_ref[i + 2]) - (f_ref[i] + f_ref[i + 3])
        )

    def row(i, carry):
        f = f_ref[i + 2]
        west, east = shift(f, 1), shift(f, -1)
        west_flux = b_ref[i + offset] * (7.0 * (west + f) - (shift(f, 2) + east))
        east_flux = c_ref[i + offset] * (7.0 * (f + east) - (west + shift(f, -2)))
        out_ref[i] = f - (face(i + 1) - face(i)) - (east_flux - west_flux)
        return carry

    lax.fori_loop(0, count, row, 0, unroll=ROW_UNROLL)


def smooth(f_ref, k_ref):
    def row(i, carry):
        k = k_ref[i]
        keep = 1.0 - 2.0 * k
        f = f_ref[i]
        near = shift(f, 1) + shift(f, -1)
        middle = shift(f, 2) + shift(f, -2)
        outer = shift(f, 3) + shift(f, -3)
        f_ref[i] = (
            (keep * keep * keep + 6.0 * keep * k * k) * f
            + (3.0 * keep * keep * k + 3.0 * k * k * k) * near
            + (3.0 * keep * k * k) * middle
            + (k * k * k) * outer
        )
        return carry

    largest = k_ref[0]
    for i in range(1, ROWS):
        largest = jnp.maximum(largest, k_ref[i])

    @pl.when(largest > 0.0)
    def _():
        lax.fori_loop(0, ROWS, row, 0, unroll=SMOOTH_UNROLL)


def emit(f_ref, store, scale_ref=None):
    lane = lax.broadcasted_iota(jnp.int32, (8, 128), 1)

    def pair(i, carry):
        even, odd = f_ref[2 * i], f_ref[2 * i + 1]
        if scale_ref is not None:
            even, odd = even * scale_ref[2 * i], odd * scale_ref[2 * i + 1]
        odd = shift(odd, 64)
        middle = jnp.where(lane < 64, even[:, WIDE - 128 :], odd[:, :128])
        base = pl.multiple_of(i * (2 * NLON), 128)
        store(base, jnp.concatenate([even[:, : WIDE - 128], middle, odd[:, 128:]], axis=1))
        return carry

    lax.fori_loop(0, ROWS // 2, pair, 0, unroll=4)


def both(x):
    return jnp.concatenate([x, x], axis=0)


def prepare_kernel(
    lat_total, row_ref, k_ref, delp_ref, wx_ref, wy_ref, north_ref, south_ref,
    thick_ref, *refs,
):
    def load(ref, before, after, put):
        widen(
            lambda at: both(ref[:, pl.ds(at, WIDE)]),
            lambda at: both(north_ref[:, pl.ds(at + before, WIDE)]),
            lambda at: both(south_ref[:, pl.ds(at + after, WIDE)]),
            put,
        )

    half, pair = HALF * NLON, 2 * NLON
    out_ref, a_ref, b_ref, c_ref, d_ref, r_ref, x_ref, f1_ref, f2_ref, sem = refs
    held = (a_ref, b_ref, c_ref, d_ref, r_ref)
    copies = [
        pltpu.make_async_copy(held[i], out_ref.at[part], sem.at[i])
        for i, part in enumerate(parts_of())
    ]
    first = row_ref[0]

    def put_x(r, x):
        x_ref[r] = x

    def put_d(r, x):
        d_ref[r] = x

    load(wy_ref, half + pair, half + pair, put_x)

    def face(i, carry):
        at = first + (i - 2)
        scale = jnp.where((at > 0) & (at < lat_total), 1.0 / 24.0, 0.0)
        a_ref[i] = scale * (x_ref[i + 1] + x_ref[i + 2])
        return carry

    lax.fori_loop(0, 13, face, 0)
    copies[0].start()
    load(wx_ref, half - pair, half, put_x)

    def east(i, carry):
        w = x_ref[i + 2]
        b_ref[i] = (1.0 / 24.0) * (shift(w, 1) + w)
        c_ref[i] = (1.0 / 24.0) * (w + shift(w, -1))
        return carry

    lax.fori_loop(0, 12, east, 0, unroll=2)
    copies[1].start()
    copies[2].start()
    load(delp_ref, 0, 0, put_d)
    copies[3].start()
    advance(d_ref, a_ref, b_ref, c_ref, f1_ref, 12, 0)
    advance(f1_ref, a_ref, b_ref, c_ref, f2_ref, 8, 2)
    smooth(f2_ref, k_ref)

    def store(base, x):
        thick_ref[:, pl.ds(base, x.shape[1])] = x[:LAYERS]

    def invert(i, carry):
        r_ref[i] = 1.0 / f2_ref[i]
        return carry

    lax.fori_loop(0, ROWS, invert, 0)
    copies[4].start()
    emit(f2_ref, store)
    for copy in copies:
        copy.wait()


def whole(*shape):
    return pl.BlockSpec(shape, lambda *_: (0,) * len(shape))


def pack_kernel(delp_ref, wx_ref, wy_ref, north_ref, south_ref):
    half, pair = HALF * NLON, 2 * NLON
    cells = delp_ref.shape[1]
    north_ref[:, :half] = delp_ref[:, :half]
    north_ref[:, half : half + pair] = wx_ref[:, :pair]
    north_ref[:, half + pair :] = wy_ref[:, :half]
    south_ref[:, :half] = delp_ref[:, half:]
    south_ref[:, half : half + pair] = wx_ref[:, cells - pair :]
    south_ref[:, half + pair :] = wy_ref[:, half:]


def pack(delp, wx, wy):
    layers, cells = delp.shape
    shape = (layers, (2 * HALF + 2) * NLON)
    return pl.pallas_call(
        pack_kernel,
        grid=(1,),
        out_shape=[jax.ShapeDtypeStruct(shape, jnp.float32)] * 2,
        in_specs=[whole(layers, cells)] * 3,
        out_specs=[whole(*shape)] * 2,
        compiler_params=params(),
        cost_estimate=SMALL,
        name="pack",
    )(delp, wx, wy)


def parts_of():
    starts = [sum(COUNTS[:i]) for i in range(len(COUNTS))]
    return [pl.ds(start, count) for start, count in zip(starts, COUNTS)]


def prepare(first_row, k, delp, wx, wy, north, south, lat_total):
    flat = whole(*delp.shape)
    halo = whole(*north.shape)
    smem = pl.BlockSpec(memory_space=pltpu.SMEM)
    return pl.pallas_call(
        functools.partial(prepare_kernel, lat_total),
        grid=(1,),
        out_shape=[jax.ShapeDtypeStruct(delp.shape, jnp.float32)]
        + [jax.ShapeDtypeStruct((sum(COUNTS), 8, WIDE), jnp.float32)],
        in_specs=[smem, smem, flat, flat, flat, halo, halo],
        out_specs=[flat, pl.BlockSpec(memory_space=pl.ANY)],
        scratch_shapes=[
            pltpu.VMEM((n, 8, WIDE), jnp.float32) for n in (*COUNTS, 16, 12, 8)
        ]
        + [pltpu.SemaphoreType.DMA((len(COUNTS),))],
        compiler_params=params(),
        cost_estimate=SMALL,
        name="prepare",
    )(first_row, k, delp, wx, wy, north, south)


def transport_kernel(with_theta, *refs):
    if with_theta:
        theta_ref, *refs = refs
    (
        k_ref, lower_ref, upper_ref, north_ref, south_ref,
        rows_ref, first_ref, last_ref, f0_ref, f1_ref, f2_ref,
        a_ref, b_ref, c_ref, d_ref, r_ref, sem,
    ) = refs
    pair = pl.program_id(0)
    held = (a_ref, b_ref, c_ref, d_ref, r_ref)
    copies = [
        pltpu.make_async_copy(rows_ref.at[part], held[i], sem.at[i])
        for i, part in enumerate(parts_of())
    ]

    @pl.when(pair == 0)
    def _():
        for i in (3, 0, 1, 2, 4):
            copies[i].start()
        copies[3].wait()

    def lower(s):
        x = lower_ref[0, :, pl.ds(s, WIDE)]
        if not with_theta:
            return x
        return jnp.where(pair == 0, theta_ref[:, pl.ds(s, WIDE)], x)

    def put(r, x):
        f0_ref[r] = x * d_ref[r]

    widen(
        lambda at: jnp.concatenate([lower(at), upper_ref[0, :, pl.ds(at, WIDE)]], axis=0),
        lambda at: jnp.concatenate(
            [north_ref[0, :, pl.ds(at, WIDE)], north_ref[1, :, pl.ds(at, WIDE)]], axis=0
        ),
        lambda at: jnp.concatenate(
            [south_ref[0, :, pl.ds(at, WIDE)], south_ref[1, :, pl.ds(at, WIDE)]], axis=0
        ),
        put,
    )

    @pl.when(pair == 0)
    def _():
        for i in (0, 1, 2, 4):
            copies[i].wait()

    advance(f0_ref, a_ref, b_ref, c_ref, f1_ref, 12, 0)
    advance(f1_ref, a_ref, b_ref, c_ref, f2_ref, 8, 2)
    smooth(f2_ref, k_ref)

    def store(base, x):
        at = pl.ds(base, x.shape[1])
        for field in range(2):
            first_ref[field, :, at] = x[LAYERS * field : LAYERS * field + 2]
            last_ref[field, :, at] = x[LAYERS * field + 2 : LAYERS * field + 4]

    emit(f2_ref, store, r_ref)


def transport(pairs, first, theta, k, tracers, north, south, rows):
    cells = tracers.shape[2]
    lead = 0 if theta is None else 1
    field = lambda index: pl.BlockSpec((1, LAYERS, cells), index)
    halo = pl.BlockSpec((2, LAYERS, HALF * NLON), lambda p: (p, 0, 0))
    in_specs = [
        pl.BlockSpec(memory_space=pltpu.SMEM),
        field(lambda p: (jnp.maximum(first + 2 * p - lead, first), 0, 0)),
        field(lambda p: (first + 2 * p + 1 - lead, 0, 0)),
        halo, halo, pl.BlockSpec(memory_space=pl.ANY),
    ]
    args = [k, tracers, tracers, north, south, rows]
    half = pl.BlockSpec((2, 2, cells), lambda p: (p, 0, 0))
    if lead:
        in_specs = [whole(*theta.shape)] + in_specs
        args = [theta] + args
    return pl.pallas_call(
        functools.partial(transport_kernel, bool(lead)),
        grid=(pairs,),
        out_shape=[jax.ShapeDtypeStruct((2 * pairs, 2, cells), jnp.float32)] * 2,
        in_specs=in_specs,
        out_specs=[half, half],
        scratch_shapes=[
            pltpu.VMEM((n, 8, WIDE), jnp.float32)
            for n in (16, 12, 8, *COUNTS)
        ]
        + [pltpu.SemaphoreType.DMA((len(COUNTS),))],
        compiler_params=params(SMALL_LIMIT),
        cost_estimate=SMALL,
        name="transport",
    )(*args)


def edges_kernel(
    rows, weight_ref, lev_ref, thick_ref,
    ov_ref, delp_ref, log_ref, choice_ref, edge_ref, flag_ref,
):
    wrapped, places = rows
    groups, _, width = thick_ref.shape
    levels = groups * LAYERS
    lev = lev_ref[0]
    sums = [jnp.float32(0.0)]
    for l in range(levels):
        sums.append(sums[-1] + weight_ref[l])
    edge = jnp.full((1, width), TOP, jnp.float32)
    marks = []
    for l in range(levels):
        edge_ref[l // LAYERS, l % LAYERS : l % LAYERS + 1] = edge
        marks.append(edge)
        edge = edge + thick_ref[l // LAYERS, l % LAYERS : l % LAYERS + 1]
    scale = (edge - TOP) / jnp.full((1, width), sums[levels], jnp.float32)
    level = lax.broadcasted_iota(jnp.int32, (LAYERS, width), 0)
    low = jnp.zeros((LAYERS, width), jnp.float32)
    high = low
    own = [sums[i] for i in range(LAYERS + 1)]
    for g in range(1, groups):
        own = [jnp.where(lev == g, sums[g * LAYERS + i], own[i]) for i in range(LAYERS + 1)]
    for i in range(LAYERS):
        low = jnp.where(level == i, own[i], low)
        high = jnp.where(level == i, own[i + 1], high)
    low, high = TOP + low * scale, TOP + high * scale
    delp = high - low
    delp_ref[...] = delp
    log_ref[...] = jnp.log(high / low)
    inverse = 1.0 / delp
    for i, (away, l) in enumerate(places):
        if wrapped:
            group = lax.rem(lev + away + groups, groups)
        else:
            group = jnp.clip(lev + away, 0, groups - 1)
        base = jnp.broadcast_to(edge_ref[group, l : l + 1], (LAYERS, width))
        limit = jnp.broadcast_to(thick_ref[group, l : l + 1], (LAYERS, width))
        part = jnp.minimum(jnp.maximum(high - base, 0.0), limit) - jnp.minimum(
            jnp.maximum(low - base, 0.0), limit
        )
        ov_ref[i] = part * inverse

    step = pl.program_id(0)

    @pl.when(step == 0)
    def _():
        flag_ref[...] = jnp.full(flag_ref.shape, -1.0, jnp.float32)

    worst = [None, None]
    for m in range(LAYERS, levels, LAYERS):
        target = TOP + sums[m] * scale
        for i in range(2):
            over = jnp.maximum(marks[m - 2 - i] - target, target - marks[m + 2 + i])
            worst[i] = over if worst[i] is None else jnp.maximum(worst[i], over)
    for i in range(2):
        best = worst[i][:, :128]
        for c in range(128, width, 128):
            best = jnp.maximum(best, worst[i][:, c : c + 128])
        flag_ref[i : i + 1] = jnp.maximum(flag_ref[i : i + 1], best)

    @pl.when(step == pl.num_programs(0) - 1)
    def _():
        two, three = jnp.max(flag_ref[0:1]), jnp.max(flag_ref[1:2])
        choice_ref[0] = jnp.where(two <= 0.0, 0, jnp.where(three <= 0.0, 1, 2))


def edges(weight, lev, thick, rows):
    groups, _, cells = thick.shape
    count = len(rows[1])
    smem = pl.BlockSpec(memory_space=pltpu.SMEM)
    own = pl.BlockSpec((LAYERS, BLOCK), lambda i: (0, i))
    level = jax.ShapeDtypeStruct((LAYERS, cells), jnp.float32)
    return pl.pallas_call(
        functools.partial(edges_kernel, rows),
        grid=(cells // BLOCK,),
        out_shape=[
            jax.ShapeDtypeStruct((count, LAYERS, cells), jnp.float32),
            level, level, jax.ShapeDtypeStruct((1,), jnp.int32),
        ],
        in_specs=[smem, smem, pl.BlockSpec((groups, LAYERS, BLOCK), lambda i: (0, 0, i))],
        out_specs=[
            pl.BlockSpec((count, LAYERS, BLOCK), lambda i: (0, 0, i)),
            own, own, smem,
        ],
        scratch_shapes=[
            pltpu.VMEM((groups, LAYERS, BLOCK), jnp.float32),
            pltpu.VMEM((8, 128), jnp.float32),
        ],
        compiler_params=params(),
        cost_estimate=SMALL,
        name="edges",
    )(weight, lev, thick)


def mix(sources, firsts, ov_ref, field):
    width = ov_ref.shape[2]
    total = None
    for density, first in zip(sources, firsts):
        for l in range(density.shape[1]):
            x = jnp.broadcast_to(density[field, l : l + 1], (LAYERS, width))
            term = x * ov_ref[first + l]
            total = term if total is None else total + term
    return total


def theta_kernel(firsts, *refs):
    n = len(firsts)
    ov_ref, log_ref, surface_ref, theta_ref, part_ref, sum_ref = refs[n:]
    theta = mix(refs[:n], firsts, ov_ref, 0)
    theta_ref[...] = theta
    column = theta * log_ref[...]
    partial = jnp.zeros((1, column.shape[1]), jnp.float32)
    for k in range(LAYERS - 1, -1, -1):
        partial = partial + column[k : k + 1]
        part_ref[k : k + 1] = partial + surface_ref[...]
    sum_ref[...] = partial


def tracer_kernel(firsts, *refs):
    n = len(firsts)
    one, two, ov_ref, out_ref = refs[:n], refs[n : 2 * n], refs[-2], refs[-1]
    for q in range(SPLIT):
        out_ref[q] = mix(two, firsts, ov_ref, q)
    for q in range(SPLIT, out_ref.shape[0]):
        out_ref[q] = mix(one, firsts, ov_ref, q - SPLIT + 1)


def flat_spec(shape, count=None):
    lead = tuple(shape[:-1]) if count is None else (count,) + tuple(shape[1:-1])
    return pl.BlockSpec(lead + (BLOCK,), lambda i: (0,) * len(lead) + (i,))


def columnwise(kernel, args, specs, outs, name):
    cells = outs[0][-1]
    return pl.pallas_call(
        kernel,
        grid=(cells // BLOCK,),
        out_shape=[jax.ShapeDtypeStruct(o, jnp.float32) for o in outs],
        in_specs=specs,
        out_specs=[flat_spec(o) for o in outs],
        compiler_params=params(),
        cost_estimate=SMALL,
        name=name,
    )(*args)


def remap_theta(sources, firsts, overlap, log_ratio, surface):
    cells = surface.shape[1]
    args = [*sources, overlap, log_ratio, surface]
    specs = [flat_spec(x.shape, 1) for x in sources]
    specs += [flat_spec(overlap.shape, used(sources)), flat_spec(log_ratio.shape)]
    specs += [flat_spec(surface.shape)]
    level = (LAYERS, cells)
    return columnwise(
        functools.partial(theta_kernel, firsts), args, specs,
        [level, level, (1, cells)], "remap_theta",
    )


def used(sources):
    return sum(x.shape[1] for x in sources)


def remap_tracers(one, two, firsts, overlap, tracers):
    args = [*one, *two]
    specs = [flat_spec(x.shape) for x in args]
    specs += [flat_spec(overlap.shape, used(one))]
    return columnwise(
        functools.partial(tracer_kernel, firsts), [*args, overlap], specs,
        [(tracers, LAYERS, overlap.shape[2])], "remap_tracers",
    )[0]


def on_device(lat_total, tracers, delp, theta, wind_x, wind_y, surface, level_weight):
    count, layers, cells = tracers.shape
    bands, groups = lax.axis_size("lat"), lax.axis_size("lev")
    band, lev = lax.axis_index("lat"), lax.axis_index("lev")
    half = HALF * NLON
    to_south = [(i, i + 1) for i in range(bands - 1)]
    to_north = [(i + 1, i) for i in range(bands - 1)]

    def beside(parts):
        last = jnp.concatenate([p[:, :, half:] for p in parts], axis=0)
        leading = jnp.concatenate([p[:, :, :half] for p in parts], axis=0)
        return exchange(leading, last)

    def exchange(leading, last):
        return lax.ppermute(last, "lat", to_south), lax.ppermute(leading, "lat", to_north)

    first_row = (band * ROWS).astype(jnp.int32)
    row_index = (first_row + jnp.arange(ROWS, dtype=jnp.int32)).astype(jnp.float32)
    latitude = jnp.pi * ((row_index + 0.5) / lat_total - 0.5)
    k = 0.25 * jnp.maximum(0.0, 1.0 - 2.0 * jnp.cos(latitude))
    north, south = exchange(*pack(delp, wind_x, wind_y))
    halo_one = beside([theta[None], tracers[SPLIT:]])
    halo_two = beside([tracers[:SPLIT]])
    ground, own_delp = lax.optimization_barrier((surface[None], delp))
    thick, rows = prepare(
        first_row[None], k, own_delp, wind_x, wind_y, north, south, lat_total
    )
    thick_all = lax.all_gather(thick, "lev", axis=0)
    down = lambda by: [(i + by, i) for i in range(groups - by)]
    up = lambda by: [(i, i + by) for i in range(groups - by)]

    def window(first, last):
        return lax.ppermute(last, "lev", up(1)), lax.ppermute(first, "lev", down(1))

    one = transport((count - SPLIT + 1) // 2, SPLIT, theta, k, tracers, *halo_one, rows)
    near_one = window(*one)
    two = transport(SPLIT // 2, 0, None, k, tracers, *halo_two, rows)
    near_two = window(*two)
    places = [(0, l) for l in range(LAYERS)]
    places += [(-1, 2), (-1, 3), (1, 0), (1, 1), (-1, 1), (1, 2)]
    overlap, new_delp, log_ratio, choice = edges(
        level_weight, lev[None], thick_all, (False, places)
    )

    def finish(one, two, firsts, overlap, log_ratio, surface):
        new_theta, partial, total = remap_theta(one, firsts, overlap, log_ratio, surface)
        above = sum(lax.ppermute(total, "lev", down(by)) for by in range(1, groups))
        new_tracers = remap_tracers(one, two, firsts, overlap, count)
        return new_tracers, new_theta, partial + above

    def reach_two(one, two, overlap, log_ratio, surface, thick_all):
        return finish(one, two, (0, 2, 4, 6), overlap, log_ratio, surface)

    def reach_three(one, two, overlap, log_ratio, surface, thick_all):
        def more(first, last, *near):
            return (first, last, *near, *window(last[:, :1], first[:, 1:]))

        firsts = (0, 2, 4, 6, 8, 9)
        return finish(more(*one), more(*two), firsts, overlap, log_ratio, surface)

    def reach_all(one, two, overlap, log_ratio, surface, thick_all):
        places = [(-by, l) for by in range(groups) for l in range(LAYERS)]
        overlap = edges(level_weight, lev[None], thick_all, (True, places))[0]

        def around(x):
            turned = [
                lax.ppermute(x, "lev", [(i, (i + by) % groups) for i in range(groups)])
                for by in range(1, groups)
            ]
            return [x, *turned]

        def spread(first, last, *near):
            return (*around(first), *around(last))

        starts = range(0, groups * LAYERS, LAYERS)
        firsts = (*starts, *(i + 2 for i in starts))
        return finish(spread(*one), spread(*two), firsts, overlap, log_ratio, surface)

    new_tracers, new_theta, geopotential = lax.switch(
        choice[0],
        [reach_two, reach_three, reach_all],
        (*one, *near_one), (*two, *near_two), overlap, log_ratio, ground, thick_all,
    )
    return new_tracers, new_theta, new_delp, geopotential


def solution(mesh):
    lat_total = ROWS * mesh.shape["lat"]
    return jax.shard_map(
        functools.partial(on_device, lat_total),
        mesh=mesh,
        in_specs=(
            P(None, "lev", "lat"),
            P("lev", "lat"),
            P("lev", "lat"),
            P("lev", "lat"),
            P("lev", "lat"),
            P("lat"),
            P(),
        ),
        out_specs=(P(None, "lev", "lat"), P("lev", "lat"), P("lev", "lat"), P("lev", "lat")),
        check_vma=False,
    )
```
